32 devices in a mesh: rows: 8 (over z, x), cols: 4 (over y, core).
Axes of the slice: x: 2, y: 2, z: 4, core: 2. Of those that a mesh axis runs over, the one named last changes fastest.
Arguments:
- features: bfloat16 [64, 128, 512], P('rows', 'cols'), may hold values from -6 to 6
- kernel: bfloat16 [4608, 512], replicated, may hold values from -0.09375 to 0.09375
- out_grad: bfloat16 [64, 128, 512], P('rows', 'cols'), may hold values from -6 to 6
- projector: bfloat16 [1024, 1024], P('rows', 'cols'), may hold values from -0.375 to 0.375
- mixers: bfloat16 [2, 128, 256], replicated, may hold values from -0.5 to 0.5
Outputs:
- output: bfloat16 [64, 128, 512], P('rows', 'cols')
- grad_features: bfloat16 [64, 128, 512], P('rows', 'cols')
- grad_kernel: float32 [9, 512, 512], P(None, 'rows', 'cols')
- sketch: bfloat16 [128, 4608], P('cols', 'rows')
The draws below stay inside these ranges and needn't reach their ends.
All inputs are finite; a program needn't handle non-finite values.
Results may differ from the reference program's by a relative error of at most 0.015.
Values may be sent and summed in bfloat16 or wider, within the bound.
No kernel may reach another device: no remote copies, remote signals or barrier semaphores. Data moves between devices by JAX's collectives and lax.ppermute only.
A program may use at most 192 MiB of HBM per device.

```python
import jax
import jax.numpy as jnp
from jax import lax

CH = 512
RANK = 128
NS_STEPS = 5
PATCH = 4608
PIX_DEV = 256
HEIGHT = 64
WIDTH = 128
ROW_LEVELS = 3
COL_LEVELS = 2
N_ROWS = 8
N_COLS = 4


def spiked(array, stream_key, source, target, parts, factor):
    owner, partner = [(jnp.arange(array.shape[dim]) // (array.shape[dim] // parts)).reshape([-1 if axis == dim else 1 for axis in range(array.ndim)]) for dim in (source, target)]
    chosen = jax.random.permutation(stream_key, parts)[partner]
    strong = (owner == chosen) | (owner == (partner + parts // 2) % parts)
    return jnp.where(strong, factor * array, array)


def shard_levels(key, shape, pieces, low, top_value):
    def one(axis_at, blocks):
        draws = jax.random.uniform(jax.random.fold_in(jax.random.fold_in(key, 6), axis_at), (blocks,), jnp.float32, low / len(pieces), top_value / len(pieces))
        return jnp.repeat(jnp.exp(draws), shape[axis_at] // blocks).reshape((-1,) + (1,) * (len(shape) - axis_at - 1))

    gain = one(*pieces[0])
    for cut in pieces[1:]:
        gain = gain * one(*cut)
    return gain


def noise(rng, shape, width, most, cuts=(), kind=jnp.bfloat16):
    result = width * jax.random.normal(rng, shape, jnp.float32)
    if cuts:
        result = result * shard_levels(rng, shape, cuts, -0.22, 0.18)
    return jnp.clip(result, -most, most).astype(kind)


def gaussian_with(stream_key, shape, deviation, most, shards, heavy, held_as=jnp.bfloat16):
    drawn = deviation * jax.random.normal(stream_key, shape, jnp.float32)
    if shards:
        drawn = drawn * shard_levels(stream_key, shape, shards, -0.22, 0.18)
    return jnp.clip(spiked(drawn, jax.random.fold_in(stream_key, 3), *heavy), -most, most).astype(held_as)


def setup_inputs(seed: int = 0) -> dict:
    streams_of = jax.random.split(jax.random.key(seed), 6)
    return {
        "features": noise(streams_of[0], (HEIGHT, WIDTH, CH), 1.0, 6.0, ((0, 8), (1, 4))),
        "kernel": noise(streams_of[1], (PATCH, CH), PATCH ** -0.5, 0.09375),
        "out_grad": gaussian_with(streams_of[2], (HEIGHT, WIDTH, CH), 1.0, 6.0, ((0, 8), (1, 4)), (0, 2, 8, 2.0)),
        "projector": noise(streams_of[3], (RANK * N_ROWS, PIX_DEV * N_COLS), PIX_DEV ** -0.5, 0.375, ((0, 8), (1, 4))),
        "mixers": noise(streams_of[4], (2, RANK, 2 * RANK), RANK ** -0.5, 0.5),
    }


def finish_merge(gram_matrix, stacked, mix_matrix):
    size_two = gram_matrix.shape[0]
    identity = jnp.eye(size_two, dtype=jnp.float32)
    spread = gram_matrix / (jnp.trace(gram_matrix) + 1e-06) - identity / size_two
    spread = spread / (jnp.sqrt(jnp.sum(spread * spread)) + 1e-06)
    for sweep in range(NS_STEPS):
        square = jnp.dot(spread, spread, precision=lax.Precision.HIGHEST)
        spread = 1.5 * spread - 0.5 * jnp.dot(spread, square, precision=lax.Precision.HIGHEST)
    keeper = 0.5 * (identity + spread)
    combiner = jnp.dot(mix_matrix.astype(jnp.float32), keeper, precision=lax.Precision.HIGHEST).astype(jnp.bfloat16)
    return jnp.dot(combiner, stacked, preferred_element_type=jnp.float32).astype(jnp.bfloat16)

def full_merge(upper_part, lower_part, mix_matrix):
    stacked = jnp.concatenate([upper_part, lower_part], axis=0)
    gram_matrix = lax.dot_general(stacked, stacked, (((1,), (1,)), ((), ())), preferred_element_type=jnp.float32)
    return finish_merge(gram_matrix, stacked, mix_matrix)

def reference(features, kernel, out_grad, projector, mixers):
    height, width_all, channels = features.shape
    band_rows = height // N_ROWS
    band_cols = width_all // N_COLS
    padded = jnp.pad(features, ((1, 1), (1, 1), (0, 0)))
    grad_padded = jnp.pad(out_grad, ((1, 1), (1, 1), (0, 0)))
    taps = kernel.reshape(9, channels, channels)
    flat_grad = out_grad.reshape(-1, channels)
    block_proj = projector.reshape(N_ROWS, RANK, N_COLS, band_rows * band_cols).astype(jnp.float32)
    forward = jnp.zeros((height * width_all, channels), jnp.float32)
    backward = jnp.zeros((height * width_all, channels), jnp.float32)
    kernel_grads = []
    sketch_parts = []
    for tap_index in range(9):
        row_tap = tap_index // 3
        col_tap = tap_index % 3
        shifted = padded[row_tap:row_tap + height, col_tap:col_tap + width_all, :]
        flat_shift = shifted.reshape(-1, channels)
        forward = forward + jnp.dot(flat_shift, taps[tap_index], preferred_element_type=jnp.float32)
        grad_shift = grad_padded[2 - row_tap:2 - row_tap + height, 2 - col_tap:2 - col_tap + width_all, :].reshape(-1, channels)
        backward = backward + jnp.dot(grad_shift, taps[tap_index].T, preferred_element_type=jnp.float32)
        kernel_grads.append(lax.dot_general(flat_shift, flat_grad, (((0,), (0,)), ((), ())), preferred_element_type=jnp.float32))
        blocks = shifted.reshape(N_ROWS, band_rows, N_COLS, band_cols, channels).transpose(0, 2, 1, 3, 4)
        blocks = blocks.reshape(N_ROWS, N_COLS, band_rows * band_cols, channels).astype(jnp.float32)
        sketch_parts.append(jnp.einsum('rlcp,rcpi->rcli', block_proj, blocks, precision=lax.Precision.HIGHEST))
    output = forward.astype(jnp.bfloat16).reshape(height, width_all, channels)
    grad_features = backward.astype(jnp.bfloat16).reshape(height, width_all, channels)
    grad_kernel = jnp.stack(kernel_grads, axis=0)
    sketches = jnp.concatenate(sketch_parts, axis=3).astype(jnp.bfloat16)
    merge_grid = jax.vmap(jax.vmap(full_merge, in_axes=(0, 0, None)), in_axes=(0, 0, None))
    for tree_level in range(ROW_LEVELS):
        sketches = merge_grid(sketches[0::2], sketches[1::2], mixers[0])
    bands = sketches[0]
    merge_line = jax.vmap(full_merge, in_axes=(0, 0, None))
    for tree_level in range(COL_LEVELS):
        bands = merge_line(bands[0::2], bands[1::2], mixers[1])
    return (output, grad_features, grad_kernel, bands[0])
```

```python
import functools
import jax
import jax.numpy as jnp
from jax import lax
from jax.experimental import pallas as pl
from jax.experimental.pallas import tpu as pltpu
from jax.sharding import PartitionSpec as P

NS_STEPS = 5
GROUP = 8
NT = (((1,), (1,)), ((), ()))
F32, BF16 = jnp.float32, jnp.bfloat16
VMEM = pl.BlockSpec(memory_space=pltpu.VMEM)
SMEM = pl.BlockSpec(memory_space=pltpu.SMEM)
ANY = pl.BlockSpec(memory_space=pl.ANY)


def mm(a, b):
    return jnp.dot(a, b, preferred_element_type=F32)


def spectral(grams):
    size = grams[0].shape[0]
    rows = lax.broadcasted_iota(jnp.int32, (size, size), 0)
    cols = lax.broadcasted_iota(jnp.int32, (size, size), 1)
    diagonal = rows == cols

    def total(x):
        return jnp.sum(jnp.sum(x, axis=1, keepdims=True), axis=0, keepdims=True)

    spreads = []
    for gram in grams:
        trace = total(jnp.where(diagonal, gram, 0.0))
        spread = gram / (trace + 1e-06) - jnp.where(diagonal, 1.0 / size, 0.0)
        spreads.append(spread / (jnp.sqrt(total(spread * spread)) + 1e-06))
    for sweep in range(NS_STEPS):
        low = [y.astype(BF16) for y in spreads]
        squares = [mm(y, y).astype(BF16) for y in low]
        spreads = [1.5 * s - 0.5 * mm(y, z) for s, y, z in zip(spreads, low, squares)]
    return spreads


def combiner(mix, spread):
    return (0.5 * (mix.astype(F32) + mm(mix, spread.astype(BF16)))).astype(BF16)


def gram_terms(parts):
    total = None
    for part in parts:
        term = lax.dot_general(part, part, NT, preferred_element_type=F32)
        total = term if total is None else total + term
    return total


def shifted(block, left, right):
    at = lax.broadcasted_iota(jnp.int32, block.shape, 0)
    wide = block.astype(F32)
    size = block.shape[0]
    low = jnp.where(at == 0, left, pltpu.roll(wide, 1, 0)).astype(BF16)
    high = jnp.where(at == size - 1, right, pltpu.roll(wide, size - 1, 0)).astype(BF16)
    return low, high


def rows_at(src, j, a):
    rows = src.shape[1]
    if a == 1:
        value = src[j]
    elif a == 0:
        value = jnp.concatenate([src[j - 1, rows - 1 : rows], src[j, : rows - 1]], axis=0)
    else:
        value = jnp.concatenate([src[j, 1:rows], src[j + 1, 0:1]], axis=0)
    return value.reshape(-1, src.shape[3])


def row_tree_kernel(step, mix_ref, proj_ref, halo_ref, band_ref, out_ref, raw, lo, hi, sk, sems):
    blocks, rows, cols, chans = raw.shape
    rank = proj_ref.shape[1]
    copies = [
        pltpu.make_async_copy(band_ref.at[j], raw.at[j], sems.at[j]) for j in range(blocks)
    ]
    for copy in copies:
        copy.start()

    def shift(j, h):
        k = j * rows + h
        lo[j, h], hi[j, h] = shifted(raw[j, h], halo_ref[0, k : k + 1], halo_ref[2, k : k + 1])

    copies[0].wait()
    shift(0, rows - 1)
    copies[1].wait()
    for h in range(rows):
        shift(1, h)
    for j in range(1, blocks - 1):
        copies[j + 1].wait()
        for h in range(rows if j + 1 < blocks - 1 else 1):
            shift(j + 1, h)
        half, part = divmod(j - 1, 2)
        for a in range(3):
            for b, src in enumerate((lo, raw, hi)):
                t = 3 * a + b
                sk[half, part * rank : (part + 1) * rank, t * chans : (t + 1) * chans] = mm(
                    proj_ref[j - 1], rows_at(src, j, a)
                ).astype(BF16)
    mix = mix_ref[...]
    count = (blocks - 2) // 2
    width = sk.shape[-1]
    starts = range(0, width, step)
    while count:
        spreads = spectral(
            [gram_terms(sk[i, :, s : s + step] for s in starts) for i in range(count)]
        )
        for i in range(count):
            mixed = combiner(mix, spreads[i])
            for s in starts:
                piece = mm(mixed, sk[i, :, s : s + step]).astype(BF16)
                if count == 1:
                    out_ref[:, s : s + step] = piece
                else:
                    sk[i // 2, (i % 2) * rank : (i % 2 + 1) * rank, s : s + step] = piece
        count //= 2


def row_tree(mix, proj, halo, band):
    blocks, rows, cols, chans = band.shape
    rank = mix.shape[0]
    width = 9 * chans
    return pl.pallas_call(
        functools.partial(row_tree_kernel, 1536),
        out_shape=jax.ShapeDtypeStruct((rank, width), BF16),
        in_specs=[VMEM, VMEM, VMEM, ANY],
        out_specs=VMEM,
        scratch_shapes=[
            pltpu.VMEM((blocks, rows, cols, chans), BF16),
            pltpu.VMEM((blocks, rows, cols, chans), BF16),
            pltpu.VMEM((blocks, rows, cols, chans), BF16),
            pltpu.VMEM(((blocks - 2) // 2, 2 * rank, width), BF16),
            pltpu.SemaphoreType.DMA((blocks,)),
        ],
        compiler_params=pltpu.CompilerParams(vmem_limit_bytes=48 << 20),
        cost_estimate=pl.CostEstimate(flops=2 * 10**10, bytes_accessed=8 << 20, transcendentals=0),
        name="row_tree",
    )(mix, proj, halo, band)


def merge_kernel(step, halves, share, where_ref, mix_ref, *refs):
    rank, width = refs[0].shape
    own = refs[0]
    others = refs[1 : 2 + halves]
    outs = refs[2 + halves :]
    half = width // 2
    core = where_ref[1]

    def spans():
        for s in range(0, width, step):
            if halves:
                which, inner = divmod(s, half)
                place = pl.multiple_of((core + which) % 2 * half + inner, 128)
                other = others[which][:, inner : inner + step]
            else:
                place, other = s, others[0][:, s : s + step]
            yield place, jnp.concatenate([own[:, pl.ds(place, step)], other], axis=0)

    spread = spectral([gram_terms(part for _, part in spans())])[0]
    if share:
        mix = mix_ref[pl.ds(pl.multiple_of(where_ref[2] * share, 16), share), :]
    else:
        mix = mix_ref[...]
    turned = jnp.concatenate([mix[:, rank:], mix[:, :rank]], axis=1)
    mix = jnp.where(where_ref[0] == 0, mix.astype(F32), turned.astype(F32)).astype(BF16)
    mixed = combiner(mix, spread)
    for place, part in spans():
        outs[0][:, pl.ds(place, step)] = mm(mixed, part).astype(BF16)
    if not share:
        outs[1][...] = outs[0][:, pl.ds(pl.multiple_of(core * half, 128), half)]


def merge(where, mix, own, others, share):
    rank, width = own.shape
    shapes = [jax.ShapeDtypeStruct((share or rank, width), BF16)]
    if not share:
        shapes.append(jax.ShapeDtypeStruct((rank, width // 2), BF16))
    return pl.pallas_call(
        functools.partial(merge_kernel, 1152, len(others) == 2, share),
        out_shape=shapes,
        in_specs=[SMEM] + [VMEM] * (2 + len(others)),
        out_specs=[VMEM] * len(shapes),
        compiler_params=pltpu.CompilerParams(vmem_limit_bytes=32 << 20),
        cost_estimate=pl.CostEstimate(flops=4 * 10**9, bytes_accessed=4 << 20, transcendentals=0),
        name="merge",
    )(where, mix, own, *others)


def conv_kernel(where_ref, kernel_ref, halo_ref, feat_ref, grad_ref, out_ref, back_ref, raw, lo, hi, total, sems):
    tap = pl.program_id(0)
    rows, cols, chans = raw.shape[2:]
    row = where_ref[0]
    arrays = (feat_ref, grad_ref)

    @pl.when(tap == 0)
    def start():
        copies = [
            pltpu.make_async_copy(ref.at[pl.ds(row, 3)], raw.at[n], sems.at[n])
            for n, ref in enumerate(arrays)
        ]
        for copy in copies:
            copy.start()
        for n, copy in enumerate(copies):
            copy.wait()
            base = pl.multiple_of(row * rows, rows)
            left = halo_ref[n, pl.ds(base, 3 * rows), :]
            right = halo_ref[2 + n, pl.ds(base, 3 * rows), :]
            for k in range(rows - 1, 2 * rows + 1):
                j, h = divmod(k, rows)
                lo[n, j, h], hi[n, j, h] = shifted(
                    raw[n, j, h], left[k : k + 1], right[k : k + 1]
                )
        total[...] = jnp.zeros_like(total)

    for a in range(3):
        for b in range(3):

            @pl.when(tap == 3 * a + b)
            def add(a=a, b=b):
                weights = kernel_ref[...]
                total[0] += mm(rows_at((lo, raw, hi)[b].at[0], 1, a), weights)
                total[1] += lax.dot_general(
                    rows_at((lo, raw, hi)[2 - b].at[1], 1, 2 - a), weights, NT, preferred_element_type=F32
                )

    @pl.when(tap == 8)
    def finish():
        out_ref[...] = total[0].astype(BF16)
        back_ref[...] = total[1].astype(BF16)


def convolutions(where, kernel, halo, feat_band, grad_band):
    rows, cols, chans = feat_band.shape[1:]
    block = jax.ShapeDtypeStruct((rows * cols, chans), BF16)
    scratch = pltpu.VMEM((2, 3, rows, cols, chans), BF16)
    whole = pl.BlockSpec((rows * cols, chans), lambda t: (0, 0))
    return pl.pallas_call(
        conv_kernel,
        grid=(9,),
        out_shape=[block, block],
        in_specs=[SMEM, pl.BlockSpec((chans, chans), lambda t: (t, 0)), VMEM, ANY, ANY],
        out_specs=[whole, whole],
        scratch_shapes=[
            scratch,
            scratch,
            scratch,
            pltpu.VMEM((2, rows * cols, chans), F32),
            pltpu.SemaphoreType.DMA((2,)),
        ],
        compiler_params=pltpu.CompilerParams(vmem_limit_bytes=32 << 20),
        cost_estimate=pl.CostEstimate(flops=5 * 10**9, bytes_accessed=8 << 20, transcendentals=0),
        name="convolutions",
    )(where, kernel, halo, feat_band, grad_band)


def ring_row(place, count):
    return jnp.where(place < count // 2, 2 * place, 2 * (count - 1 - place) + 1)


def ring_place(row, count):
    return jnp.where(row % 2 == 0, row // 2, count - 1 - row // 2)


def body(features, kernel, out_grad, projector, mixers):
    rows, cols, chans = features.shape
    row_count, col_count = lax.axis_size("rows"), lax.axis_size("cols")
    row, col = lax.axis_index("rows"), lax.axis_index("cols")
    rank = projector.shape[0]
    core = col % 2

    order = list(range(0, row_count, 2)) + list(range(row_count - 1, 0, -2))
    ahead = [(order[i], order[(i + 1) % row_count]) for i in range(row_count)]
    behind = [(j, i) for i, j in ahead]
    east = [(i, i + 1) for i in range(col_count - 1)]
    west = [(j, i) for i, j in east]

    first = jnp.stack([features[:, 0], out_grad[:, 0]])
    last = jnp.stack([features[:, cols - 1], out_grad[:, cols - 1]])
    halo = jnp.concatenate(
        [lax.ppermute(last, "cols", east), lax.ppermute(first, "cols", west)], axis=0
    )

    place = ring_place(row, row_count)
    feat_band = jnp.zeros((row_count + 2, rows, cols, chans), BF16)
    grad_band = jnp.zeros((row_count + 2, rows, cols, chans), BF16)
    halo_band = jnp.zeros((4, (row_count + 2) * rows, chans), F32)
    proj_band = jnp.zeros((row_count,) + projector.shape, BF16)

    def put_map(band, value, at, offset=0):
        return lax.dynamic_update_slice(band, value[None], (at + 1, offset, 0, 0))

    def put_halo(band, value, at):
        return lax.dynamic_update_slice(band, value.astype(F32), (0, (at + 1) * rows, 0))

    def put_proj(band, value, at):
        return lax.dynamic_update_slice(band, value[None], (at, 0, 0))

    feat_band = put_map(feat_band, features, row)
    grad_band = put_map(grad_band, out_grad, row)
    halo_band = put_halo(halo_band, halo, row)
    proj_band = put_proj(proj_band, projector, row)
    up = [features, projector, halo, out_grad]
    down = list(up)
    for step in range(1, row_count // 2):
        up = [lax.ppermute(x, "rows", ahead) for x in up]
        down = [lax.ppermute(x, "rows", behind) for x in down]
        for got, at in ((up, (place - step) % row_count), (down, (place + step) % row_count)):
            at = ring_row(at, row_count)
            feat_band = put_map(feat_band, got[0], at)
            proj_band = put_proj(proj_band, got[1], at)
            halo_band = put_halo(halo_band, got[2], at)
            grad_band = put_map(grad_band, got[3], at)
    at = ring_row((place + row_count // 2) % row_count, row_count)
    mid = rows // 2
    feat_band = put_map(feat_band, lax.ppermute(up[0][:mid], "rows", ahead), at)
    feat_band = put_map(feat_band, lax.ppermute(down[0][mid:], "rows", behind), at, mid)
    proj_band = put_proj(proj_band, lax.ppermute(up[1], "rows", ahead), at)
    halo_band = put_halo(halo_band, lax.ppermute(down[2], "rows", behind), at)
    grad_band = put_map(grad_band, lax.ppermute(up[3][:mid], "rows", ahead), at)
    grad_band = put_map(grad_band, lax.ppermute(down[3][mid:], "rows", behind), at, mid)

    where_rows = jnp.stack([row]).astype(jnp.int32)
    output, grad_features = convolutions(where_rows, kernel, halo_band, feat_band, grad_band)

    share = chans // row_count
    sliced = lax.dynamic_slice_in_dim(feat_band, row * share, share, axis=3)
    sliced = sliced.reshape((row_count + 2) * rows, cols, share)
    ends = lax.dynamic_slice_in_dim(halo_band, row * share, share, axis=2).astype(BF16)
    padded = jnp.concatenate([ends[0][:, None], sliced, ends[2][:, None]], axis=1)
    height = row_count * rows
    patches = jnp.concatenate(
        [
            padded[rows - 1 + a : rows - 1 + a + height, b : b + cols]
            for a in range(3)
            for b in range(3)
        ],
        axis=2,
    ).reshape(height * cols, 9 * share)
    flat_grad = grad_band[1 : row_count + 1].reshape(height * cols, chans)
    terms = lax.dot_general(
        patches, flat_grad, (((0,), (0,)), ((), ())), preferred_element_type=F32
    ).reshape(9, share, col_count, chans // col_count)
    for level in range(col_count.bit_length() - 1):
        bit = col >> level & 1
        pairs = terms.reshape(9, share, -1, 2, chans // col_count)
        keep = lax.dynamic_index_in_dim(pairs, bit, 3, keepdims=False)
        give = lax.dynamic_index_in_dim(pairs, 1 - bit, 3, keepdims=False).astype(BF16)
        perm = [(i, i ^ 1 << level) for i in range(col_count)]
        terms = keep + lax.ppermute(give, "cols", perm).astype(F32)
    grad_kernel = terms.reshape(9, share, chans // col_count)

    groups = []
    for start in range(0, row_count, GROUP):
        groups.append(
            row_tree(
                mixers[0],
                proj_band[start : start + GROUP],
                halo_band[:, start * rows : (start + GROUP + 2) * rows],
                feat_band[start : start + GROUP + 2],
            )
        )
    zero = jnp.zeros((), jnp.int32)
    while len(groups) > 1:
        where = jnp.stack([zero, core, col]).astype(jnp.int32)
        groups = [
            merge(where, mixers[0], groups[i], [groups[i + 1]], 0)[0]
            for i in range(0, len(groups), 2)
        ]
    sketch = groups[0]
    sibling = [(i, i ^ 1) for i in range(col_count)]
    levels = col_count.bit_length() - 1
    for level in range(levels):
        perm = [(i, i ^ 1 << level) for i in range(col_count)]
        where = jnp.stack([col >> level & 1, core, col]).astype(jnp.int32)
        if level:
            mine = lax.ppermute(half, "cols", perm)
            others = [mine, lax.ppermute(mine, "cols", sibling)]
        else:
            others = [lax.ppermute(sketch, "cols", perm)]
        last = level == levels - 1
        result = merge(where, mixers[1], sketch, others, rank // col_count if last else 0)
        if last:
            sketch = result[0]
        else:
            sketch, half = result
    patch_share = sketch.shape[1] // row_count
    own_block = lax.dynamic_slice_in_dim(sketch, row * patch_share, patch_share, axis=1)
    return (
        output.reshape(features.shape),
        grad_features.reshape(features.shape),
        grad_kernel,
        own_block,
    )


def solution(mesh):
    in_specs = (P("rows", "cols", None), P(), P("rows", "cols", None), P("rows", "cols"), P())
    out_specs = (
        P("rows", "cols", None),
        P("rows", "cols", None),
        P(None, "rows", "cols"),
        P("cols", "rows"),
    )
    return jax.shard_map(body, mesh=mesh, in_specs=in_specs, out_specs=out_specs, check_vma=False)
```

```python
import functools
import jax
import jax.numpy as jnp
from jax import lax
from jax.experimental import pallas as pl
from jax.experimental.pallas import tpu as pltpu
from jax.sharding import PartitionSpec as P

NS_STEPS = 5
GROUP = 8
NT = (((1,), (1,)), ((), ()))
F32, BF16 = jnp.float32, jnp.bfloat16
VMEM = pl.BlockSpec(memory_space=pltpu.VMEM)
SMEM = pl.BlockSpec(memory_space=pltpu.SMEM)
ANY = pl.BlockSpec(memory_space=pltpu.HBM)


def mm(a, b):
    return jnp.dot(a, b, preferred_element_type=F32)


def spectral(grams):
    size = grams[0].shape[0]
    rows = lax.broadcasted_iota(jnp.int32, (size, size), 0)
    cols = lax.broadcasted_iota(jnp.int32, (size, size), 1)
    diagonal = rows == cols

    def total(x):
        return jnp.sum(jnp.sum(x, axis=1, keepdims=True), axis=0, keepdims=True)

    spreads = []
    for gram in grams:
        trace = total(jnp.where(diagonal, gram, 0.0))
        spread = gram / (trace + 1e-06) - jnp.where(diagonal, 1.0 / size, 0.0)
        spreads.append(spread / (jnp.sqrt(total(spread * spread)) + 1e-06))
    for sweep in range(NS_STEPS):
        low = [y.astype(BF16) for y in spreads]
        squares = [mm(y, y).astype(BF16) for y in low]
        spreads = [1.5 * s - 0.5 * mm(y, z) for s, y, z in zip(spreads, low, squares)]
    return spreads


def combiner(mix, spread):
    return (0.5 * (mix.astype(F32) + mm(mix, spread.astype(BF16)))).astype(BF16)


def gram_terms(parts):
    total = None
    for part in parts:
        term = lax.dot_general(part, part, NT, preferred_element_type=F32)
        total = term if total is None else total + term
    return total


def shifted(block, left, right):
    at = lax.broadcasted_iota(jnp.int32, block.shape, 0)
    wide = block.astype(F32)
    size = block.shape[0]
    low = jnp.where(at == 0, left, pltpu.roll(wide, 1, 0)).astype(BF16)
    high = jnp.where(at == size - 1, right, pltpu.roll(wide, size - 1, 0)).astype(BF16)
    return low, high


def rows_at(src, j, a, cols):
    size = src.shape[1]
    if a == 1:
        return src[j]
    if a == 0:
        return jnp.concatenate([src[j - 1, size - cols : size], src[j, : size - cols]], axis=0)
    return jnp.concatenate([src[j, cols:size], src[j + 1, :cols]], axis=0)


def shift_row(raw, lo, hi, h, cols, side, n=0):
    rows = side.shape[0] // 4
    at = slice(h * cols, (h + 1) * cols)
    left, right = n * rows + h, (2 + n) * rows + h
    lo[at], hi[at] = shifted(raw[at], side[left : left + 1], side[right : right + 1])


def placed(values):
    return [pltpu.with_memory_space_constraint(x, pltpu.HBM) for x in values]


def start_map(refs, i, target, sem, cut=slice(None)):
    size = target.shape[0]
    if i < len(refs) - 2:
        pltpu.make_async_copy(refs[i].at[pl.ds(0, size), cut], target, sem).start()
    else:
        mid = refs[-1].shape[0]
        pltpu.make_async_copy(refs[-2].at[:, cut], target.at[pl.ds(0, mid)], sem).start()
        pltpu.make_async_copy(refs[-1].at[pl.ds(0, size - mid), cut], target.at[pl.ds(mid, size - mid)], sem).start()


def start_rest(refs, i, ends, sem, cut=slice(None), proj=None, proj_sem=None):
    ref = refs[i] if i < len(refs) - 2 else refs[-1]
    size = ends.shape[0]
    below = ref.shape[0] - size
    if proj is None:
        pltpu.make_async_copy(ref.at[pl.ds(below, size), cut], ends, sem).start()
        return
    rank, pixels = proj.shape
    packed = rank * pixels // ref.shape[1]
    below -= packed
    for n in range(rank // packed):
        part = ref.at[pl.ds(below, packed), pl.ds(n * pixels, pixels)]
        pltpu.make_async_copy(part, proj.at[pl.ds(n * packed, packed)], proj_sem).start()


def arrived(target, sem):
    pltpu.make_async_copy(target, target, sem).wait()


def row_tree_kernel(first, step, rows, rows_ref, mix_ref, *refs):
    feats = refs[:-8]
    count = len(feats) - 1
    out_ref, raw, lo, hi, ends, proj, sk, sems = refs[-8:]
    blocks, pixels, chans = raw.shape
    cols = pixels // rows
    rank = proj.shape[1]

    for i in range(count):
        j = rows_ref[i] - first + 1

        @pl.when((j >= 0) & (j < blocks))
        def fetch(i=i, j=j):
            start_map(feats, i, raw.at[j], sems.at[0, j])
            start_rest(feats, i, ends.at[j], sems.at[1, j])

        @pl.when((j >= 1) & (j < blocks - 1))
        def fetch_projector(i=i, j=j):
            start_rest(feats, i, ends.at[j], None, slice(None), proj.at[j], sems.at[2, j])

    def ready(j, wanted):
        if 0 <= first + j - 1 < count:
            arrived(raw.at[j], sems.at[0, j])
            arrived(ends.at[j], sems.at[1, j])
            side = ends[j].astype(F32)
            for h in wanted:
                shift_row(raw.at[j], lo.at[j], hi.at[j], h, cols, side)
        else:
            for h in wanted:
                for ref in (raw, lo, hi):
                    ref[j, h * cols : (h + 1) * cols] = jnp.zeros((cols, chans), BF16)

    ready(0, (rows - 1,))
    ready(1, range(rows))
    for j in range(1, blocks - 1):
        ready(j + 1, range(rows) if j + 1 < blocks - 1 else (0,))
        arrived(proj.at[j], sems.at[2, j])
        half, part = divmod(j - 1, 2)
        for a in range(3):
            for b, src in enumerate((lo, raw, hi)):
                t = 3 * a + b
                sk[half, part * rank : (part + 1) * rank, t * chans : (t + 1) * chans] = mm(
                    proj[j], rows_at(src, j, a, cols)
                ).astype(BF16)
    mix = mix_ref[...]
    left = (blocks - 2) // 2
    width = sk.shape[-1]
    starts = range(0, width, step)
    while left:
        spreads = spectral(
            [gram_terms(sk[i, :, s : s + step] for s in starts) for i in range(left)]
        )
        for i in range(left):
            mixed = combiner(mix, spreads[i])
            for s in starts:
                piece = mm(mixed, sk[i, :, s : s + step]).astype(BF16)
                if left == 1:
                    out_ref[:, s : s + step] = piece
                else:
                    sk[i // 2, (i % 2) * rank : (i % 2 + 1) * rank, s : s + step] = piece
        left //= 2


def row_tree(slots, mix, feats, first, rows, pixels):
    chans = feats[0].shape[1]
    rank = mix.shape[0]
    width = 9 * chans
    blocks = GROUP + 2
    maps = pltpu.VMEM((blocks, pixels, chans), BF16)
    return pl.pallas_call(
        functools.partial(row_tree_kernel, first, 1536, rows),
        out_shape=jax.ShapeDtypeStruct((rank, width), BF16),
        in_specs=[SMEM, VMEM] + [ANY] * len(feats),
        out_specs=VMEM,
        scratch_shapes=[
            maps,
            maps,
            maps,
            pltpu.VMEM((blocks, 4 * rows, chans), BF16),
            pltpu.VMEM((blocks, rank, pixels), BF16),
            pltpu.VMEM((GROUP // 2, 2 * rank, width), BF16),
            pltpu.SemaphoreType.DMA((3, blocks)),
        ],
        compiler_params=pltpu.CompilerParams(vmem_limit_bytes=48 << 20),
        cost_estimate=pl.CostEstimate(flops=2 * 10**10, bytes_accessed=8 << 20, transcendentals=0),
        name="row_tree",
    )(slots, mix, *placed(feats))


def own_columns(where_ref, own, others, mixed, out_ref):
    share = out_ref.shape[1]
    half = own.shape[1] // 2
    window = (share + 2 * 127) // 128 * 128
    start = where_ref[3] * share
    which = start // half
    inner = start - which * half
    base = pl.multiple_of(jnp.minimum(inner // 128 * 128, half - window), 128)
    core = where_ref[1]
    near = others[0][:, pl.ds(base, window)].astype(F32)
    far = others[1][:, pl.ds(base, window)].astype(F32)
    other = jnp.where(core == which, near, far).astype(BF16)
    part = jnp.concatenate([own[:, pl.ds(pl.multiple_of(which * half + base, 128), window)], other], axis=0)
    value = mm(mixed, part)
    value = pltpu.roll(value, (window - (inner - base)) % window, 1)
    out_ref[...] = value[:, :share].astype(BF16)


def merge_kernel(step, halves, share, where_ref, mix_ref, *refs):
    rank, width = refs[0].shape
    own = refs[0]
    others = refs[1 : 2 + halves]
    outs = refs[2 + halves :]
    if not share:
        *outs, merged, sem = outs
    half = width // 2
    core = where_ref[1]

    def spans():
        for s in range(0, width, step):
            if halves:
                which, inner = divmod(s, half)
                place = pl.multiple_of((core + which) % 2 * half + inner, 128)
                other = others[which][:, inner : inner + step]
            else:
                place, other = s, others[0][:, s : s + step]
            yield place, jnp.concatenate([own[:, pl.ds(place, step)], other], axis=0)

    spread = spectral([gram_terms(part for _, part in spans())])[0]
    if share:
        mix = mix_ref[pl.ds(pl.multiple_of(where_ref[2] * share, 16), share), :]
    else:
        mix = mix_ref[...]
    turned = jnp.concatenate([mix[:, rank:], mix[:, :rank]], axis=1)
    mix = jnp.where(where_ref[0] == 0, mix.astype(F32), turned.astype(F32)).astype(BF16)
    mixed = combiner(mix, spread)
    if share:
        own_columns(where_ref, own, others, mixed, outs[0])
        return
    for place, part in spans():
        merged[:, pl.ds(place, step)] = mm(mixed, part).astype(BF16)
    copy = pltpu.make_async_copy(merged, outs[0], sem)
    copy.start()
    outs[1][...] = merged[:, pl.ds(pl.multiple_of(core * half, 128), half)]
    copy.wait()


def merge(where, mix, own, others, share=None):
    rank, width = own.shape
    if share:
        shapes = [jax.ShapeDtypeStruct(share, BF16)]
    else:
        shapes = [pltpu.HBM((rank, width), BF16), jax.ShapeDtypeStruct((rank, width // 2), BF16)]
    return pl.pallas_call(
        functools.partial(merge_kernel, 1152, len(others) == 2, share[0] if share else 0),
        out_shape=shapes,
        in_specs=[SMEM] + [VMEM] * (2 + len(others)),
        out_specs=[VMEM] if share else [ANY, VMEM],
        scratch_shapes=() if share else (pltpu.VMEM((rank, width), BF16), pltpu.SemaphoreType.DMA),
        compiler_params=pltpu.CompilerParams(vmem_limit_bytes=16 << 20),
        cost_estimate=pl.CostEstimate(flops=4 * 10**9, bytes_accessed=4 << 20, transcendentals=0),
        name="merge",
    )(where, mix, own, *others)


def conv_kernel(rows, slots_ref, kernel_ref, *refs):
    count = (len(refs) - 9) // 2 - 1
    feats, grads = refs[: count + 1], refs[count + 1 : 2 * count + 2]
    out_ref, back_ref, raw, lo, hi, ends, weights, total, sems = refs[-9:]
    pixels, chans = raw.shape[2:]
    cols = pixels // rows
    row = slots_ref[0]
    for i in range(count):
        j = slots_ref[i] - row + 1

        @pl.when((j >= 0) & (j < 3))
        def fetch(i=i, j=j):
            start_map(feats, i, raw.at[0, j], sems.at[0, j])
            start_rest(feats, i, ends.at[j], sems.at[2, j])
            start_map(grads, i, raw.at[1, j], sems.at[1, j])

    for t in range(9):
        pltpu.make_async_copy(
            kernel_ref.at[pl.ds(t * chans, chans)], weights.at[t], sems.at[3, t]
        ).start()

    def waits(n, j):
        arrived(raw.at[n, j], sems.at[n, j])
        if n == 0:
            arrived(ends.at[j], sems.at[2, j])

    for n, out in enumerate((out_ref, back_ref)):
        for j, inside in ((0, row > 0), (2, row < count - 1)):

            @pl.when(jnp.logical_not(inside))
            def clear(n=n, j=j):
                raw[n, j] = jnp.zeros((pixels, chans), BF16)
                if n == 0:
                    ends[j] = jnp.zeros(ends.shape[1:], BF16)

            pl.when(inside)(functools.partial(waits, n, j))
        waits(n, 1)
        sides = [ends[j].astype(F32) for j in range(3)]
        for k in range(rows - 1, 2 * rows + 1):
            j, h = divmod(k, rows)
            shift_row(raw.at[n, j], lo.at[n, j], hi.at[n, j], h, cols, sides[j], n)
        for t in range(9):
            a, b = divmod(t, 3)
            if n == 0:
                arrived(weights.at[t], sems.at[3, t])
                term = mm(rows_at((lo, raw, hi)[b].at[n], 1, a, cols), weights[t])
            else:
                term = lax.dot_general(
                    rows_at((lo, raw, hi)[2 - b].at[n], 1, 2 - a, cols),
                    weights[t],
                    NT,
                    preferred_element_type=F32,
                )
            total[...] = total[...] + term if t else term
        out[...] = total[...].astype(BF16)


def convolutions(slots, kernel, feats, grads, rows):
    pixels, chans = grads[0].shape
    block = jax.ShapeDtypeStruct((pixels, chans), BF16)
    scratch = pltpu.VMEM((2, 3, pixels, chans), BF16)
    inputs = [kernel] + feats + grads
    return pl.pallas_call(
        functools.partial(conv_kernel, rows),
        out_shape=[block, block],
        in_specs=[SMEM] + [ANY] * len(inputs),
        out_specs=[VMEM, VMEM],
        scratch_shapes=[
            scratch,
            scratch,
            scratch,
            pltpu.VMEM((3, 4 * rows, chans), BF16),
            pltpu.VMEM((9, chans, chans), BF16),
            pltpu.VMEM((pixels, chans), F32),
            pltpu.SemaphoreType.DMA((4, 9)),
        ],
        compiler_params=pltpu.CompilerParams(vmem_limit_bytes=20 << 20),
        cost_estimate=pl.CostEstimate(flops=6 * 10**9, bytes_accessed=8 << 20, transcendentals=0),
        name="convolutions",
    )(slots, *placed(inputs))


def filter_kernel(group, rows, where_ref, slots_ref, *refs):
    count = (len(refs) - 9) // 2 - 1
    feats, grads = refs[: count + 1], refs[count + 1 : 2 * count + 2]
    keep_ref, give_ref, raw, lo, hi, ends, grad, total, sems = refs[-9:]
    pixels, lanes = raw.shape[1:]
    cols = pixels // rows
    pieces, taps, share, width = keep_ref.shape
    base = slots_ref[0] * share
    window = pl.multiple_of(base // lanes * lanes, lanes)
    inner = pl.multiple_of(base % lanes, 8)
    core = where_ref[1]
    cut = pl.ds(window, lanes)
    for i in range(count):
        j = slots_ref[i] + 1
        start_map(feats, i, raw.at[j], sems.at[0], cut)
        start_rest(feats, i, ends.at[j], sems.at[1], cut)
        start_map(grads, i, grad.at[j - 1], sems.at[2])
    inside = pl.ds(1, count)
    arrived(raw.at[inside], sems.at[0])
    arrived(ends.at[inside], sems.at[1])
    for j, h in ((0, rows - 1), (count + 1, 0)):
        for ref in (raw, lo, hi):
            ref[j, h * cols : (h + 1) * cols] = jnp.zeros((cols, lanes), BF16)
    for j in range(1, count + 1):
        side = ends[j].astype(F32)
        for h in range(rows):
            shift_row(raw.at[j], lo.at[j], hi.at[j], h, cols, side)
    arrived(grad, sems.at[2])
    chans = grad.shape[2]
    maps = [ref.reshape((count + 2) * pixels, lanes) for ref in (lo, raw, hi)]
    for a in range(3):
        for b, src in enumerate(maps):
            t = 3 * a + b
            for g in range(0, count, group):
                start = pixels * (g + 1) + (a - 1) * cols
                term = lax.dot_general(
                    src[start : start + group * pixels],
                    grad[g : g + group].reshape(group * pixels, chans),
                    (((0,), (0,)), ((), ())),
                    preferred_element_type=F32,
                )
                if g:
                    total[...] += term
                else:
                    total[...] = term
            mine = total[pl.ds(inner, share), :]
            for i in range(pieces):
                even = mine[:, 2 * i * width : (2 * i + 1) * width]
                odd = mine[:, (2 * i + 1) * width : (2 * i + 2) * width]
                keep_ref[i, t] = jnp.where(core == 0, even, odd)
                give_ref[i, t] = jnp.where(core == 0, odd, even).astype(BF16)


def filter_terms(where, slots, feats, grads, rows, share, col_count):
    pixels, chans = grads[0].shape
    count = len(feats) - 1
    lanes = 128
    shape = (col_count // 2, 9, share, chans // col_count)
    window = pltpu.VMEM((count + 2, pixels, lanes), BF16)
    inputs = feats + grads
    return pl.pallas_call(
        functools.partial(filter_kernel, GROUP, rows),
        out_shape=[jax.ShapeDtypeStruct(shape, F32), jax.ShapeDtypeStruct(shape, BF16)],
        in_specs=[SMEM, SMEM] + [ANY] * len(inputs),
        out_specs=[VMEM, VMEM],
        scratch_shapes=[
            window,
            window,
            window,
            pltpu.VMEM((count + 2, 4 * rows, lanes), BF16),
            pltpu.VMEM((count, pixels, chans), BF16),
            pltpu.VMEM((lanes, chans), F32),
            pltpu.SemaphoreType.DMA((3,)),
        ],
        compiler_params=pltpu.CompilerParams(vmem_limit_bytes=(8 + count) << 20),
        cost_estimate=pl.CostEstimate(flops=5 * 10**9, bytes_accessed=4 << 20, transcendentals=0),
        name="filter_terms",
    )(where, slots, *placed(inputs))


def ring_row(place, count):
    return jnp.where(place < count // 2, 2 * place, 2 * (count - 1 - place) + 1)


def ring_place(row, count):
    return jnp.where(row % 2 == 0, row // 2, count - 1 - row // 2)


def after(value, *earlier):
    return lax.optimization_barrier((value,) + earlier)[0]


def body(features, kernel, out_grad, projector, mixers):
    rows, cols, chans = features.shape
    row_count, col_count = lax.axis_size("rows"), lax.axis_size("cols")
    row, col = lax.axis_index("rows"), lax.axis_index("cols")
    rank = projector.shape[0]
    levels = col_count.bit_length() - 1
    half_way, pixels = row_count // 2, rows * cols

    order = list(range(0, row_count, 2)) + list(range(row_count - 1, 0, -2))
    east = [(i, i + 1) for i in range(col_count - 1)]
    west = [(j, i) for i, j in east]
    steps = [0] + [d for s in range(1, half_way) for d in (-s, s)] + [half_way]
    place = ring_place(row, row_count)
    slots = jnp.stack([ring_row((place + d) % row_count, row_count) for d in steps]).astype(jnp.int32)
    where = jnp.stack([row, col % 2, col, row]).astype(jnp.int32)

    def send(value, d):
        hop = [(order[i], order[(i + d) % row_count]) for i in range(row_count)]
        return lax.ppermute(value, "rows", hop)

    packed = rank * pixels // chans
    tail = jnp.concatenate([projector[n : n + packed] for n in range(0, rank, packed)], axis=1)
    own_grad = out_grad.reshape(pixels, chans)
    flat = features.reshape(pixels, chans)
    near = []
    for at, perm in ((cols - 1, east), (0, west)):
        edge = jnp.concatenate([x[at : at + pixels - cols + 1 : cols] for x in (flat, own_grad)])
        near.append(lax.ppermute(edge, "cols", perm))
    size = pixels + packed
    message = jnp.pad(jnp.concatenate([flat, tail], axis=0), ((0, 4 * rows), (0, 0)))
    message = lax.dynamic_update_slice(message, jnp.concatenate(near, axis=0), (size, 0))
    feats = {0: message}
    for s in range(1, half_way):
        for d in (1, -1):
            feats[-s * d] = send(feats[(1 - s) * d], d)
    top, bottom = lax.optimization_barrier((feats[1 - half_way], feats[half_way - 1]))
    mid = message.shape[0] // 2
    feats[half_way] = [send(top[:mid], 1), send(bottom[mid:], -1)]

    grads = {0: own_grad}
    late_grad = after(own_grad, top, bottom)
    for d in (1, 2):
        grads[-d], grads[d] = send(late_grad, d), send(late_grad, -d)

    def listed(found, split=False):
        values = [found[d] for d in steps]
        return values[:-1] + list(values[-1]) if split else values

    feats = listed(feats, True)
    groups = [
        row_tree(slots, mixers[0], feats, start, rows, pixels)
        for start in range(0, row_count, GROUP)
    ]
    while len(groups) > 1:
        straight = where.at[0].set(0)
        groups = [
            merge(straight, mixers[0], groups[i], [groups[i + 1]])[0]
            for i in range(0, len(groups), 2)
        ]
    sketch = groups[0]

    def swap(value, level):
        return lax.ppermute(value, "cols", [(i, i ^ 1 << level) for i in range(col_count)])

    def turn(level):
        return where.at[0].set(col >> level & 1)

    swapped = swap(after(sketch, grads[1], grads[-1], grads[2], grads[-2]), 0)
    top, bottom, _ = lax.optimization_barrier((grads[-2], grads[2], sketch))
    grads[-2], grads[2] = top, bottom
    for s in range(3, half_way):
        for d in (1, -1):
            grads[-s * d] = send(grads[(1 - s) * d], d)
    split, reach = pixels // 2, half_way - 2
    grads[half_way] = [send(top[:split], reach), send(bottom[split:], -reach)]
    result = merge(turn(0), mixers[1], sketch, [swapped])
    sketch, half = result
    grads = listed(grads, True)

    output, grad_features = convolutions(
        after(slots, half), kernel, feats, grads, rows
    )
    share = chans // row_count
    terms, give = filter_terms(
        after(where, grad_features), slots, feats, grads, rows, share, col_count
    )
    filtered = give
    for level in range(levels):
        if level:
            pairs = terms.reshape((-1, 2) + terms.shape[1:])
            bit = col >> level & 1
            terms = lax.dynamic_index_in_dim(pairs, bit, 1, keepdims=False)
            give = lax.dynamic_index_in_dim(pairs, 1 - bit, 1, keepdims=False).astype(BF16)
        got = swap(give, level)
        if level < levels - 1:
            terms = terms + got.astype(F32)

    for level in range(1, levels):
        mine = swap(half, level)
        if level == 1:
            mine = after(mine, filtered)
        others = [mine, swap(mine, 0)]
        final = level == levels - 1
        share = (rank // col_count, sketch.shape[1] // row_count) if final else None
        result = merge(turn(level), mixers[1], sketch, others, share)
        sketch = result[0]
        if not final:
            half = result[1]
    grad_kernel = (terms + after(got, sketch).astype(F32))[0]
    return (
        output.reshape(features.shape),
        grad_features.reshape(features.shape),
        grad_kernel,
        sketch,
    )


def solution(mesh):
    in_specs = (P("rows", "cols", None), P(), P("rows", "cols", None), P("rows", "cols"), P())
    out_specs = (
        P("rows", "cols", None),
        P("rows", "cols", None),
        P(None, "rows", "cols"),
        P("cols", "rows"),
    )
    return jax.shard_map(body, mesh=mesh, in_specs=in_specs, out_specs=out_specs, check_vma=False)
```

```python
import functools
import jax
import jax.numpy as jnp
from jax import lax
from jax.experimental import pallas as pl
from jax.experimental.pallas import tpu as pltpu
from jax.sharding import PartitionSpec as P

NS_STEPS = 5
GROUP = 8
NT = (((1,), (1,)), ((), ()))
F32, BF16 = jnp.float32, jnp.bfloat16
VMEM = pl.BlockSpec(memory_space=pltpu.VMEM)
SMEM = pl.BlockSpec(memory_space=pltpu.SMEM)
ANY = pl.BlockSpec(memory_space=pltpu.HBM)


def mm(a, b):
    return jnp.dot(a, b, preferred_element_type=F32)


def spectral(grams):
    size = grams[0].shape[0]
    rows = lax.broadcasted_iota(jnp.int32, (size, size), 0)
    cols = lax.broadcasted_iota(jnp.int32, (size, size), 1)
    diagonal = rows == cols

    def total(x):
        return jnp.sum(jnp.sum(x, axis=1, keepdims=True), axis=0, keepdims=True)

    spreads = []
    for gram in grams:
        trace = total(jnp.where(diagonal, gram, 0.0))
        spread = gram / (trace + 1e-06) - jnp.where(diagonal, 1.0 / size, 0.0)
        spreads.append(spread / (jnp.sqrt(total(spread * spread)) + 1e-06))
    for sweep in range(NS_STEPS - 1):
        low = [y.astype(BF16) for y in spreads]
        squares = [mm(y, y).astype(BF16) for y in low]
        spreads = [1.5 * s - 0.5 * mm(y, z) for s, y, z in zip(spreads, low, squares)]
    return spreads


def combiner(mix, spread):
    low = spread.astype(BF16)
    square = mm(low, low).astype(BF16)
    once = mm(mix, low)
    turned = 1.5 * once - 0.5 * mm(once.astype(BF16), square)
    return (0.5 * (mix.astype(F32) + turned)).astype(BF16)


def gram_terms(parts):
    total = None
    for part in parts:
        term = lax.dot_general(part, part, NT, preferred_element_type=F32)
        total = term if total is None else total + term
    return total


def shifted(block, left, right):
    at = lax.broadcasted_iota(jnp.int32, block.shape, 0)
    wide = block.astype(F32)
    size = block.shape[0]
    low = jnp.where(at == 0, left, pltpu.roll(wide, 1, 0)).astype(BF16)
    high = jnp.where(at == size - 1, right, pltpu.roll(wide, size - 1, 0)).astype(BF16)
    return low, high


def rows_at(src, j, a, cols):
    size = src.shape[1]
    if a == 1:
        return src[j]
    if a == 0:
        return jnp.concatenate([src[j - 1, size - cols : size], src[j, : size - cols]], axis=0)
    return jnp.concatenate([src[j, cols:size], src[j + 1, :cols]], axis=0)


def shift_row(raw, lo, hi, h, cols, side, n=0):
    rows = side.shape[0] // 4
    at = slice(h * cols, (h + 1) * cols)
    left, right = n * rows + h, (2 + n) * rows + h
    lo[at], hi[at] = shifted(raw[at], side[left : left + 1], side[right : right + 1])


def placed(values):
    return [pltpu.with_memory_space_constraint(x, pltpu.HBM) for x in values]


def start_map(refs, i, target, sem, cut=slice(None)):
    size = target.shape[0]
    if i < len(refs) - 2:
        pltpu.make_async_copy(refs[i].at[pl.ds(0, size), cut], target, sem).start()
    else:
        mid = refs[-1].shape[0]
        pltpu.make_async_copy(refs[-2].at[:, cut], target.at[pl.ds(0, mid)], sem).start()
        pltpu.make_async_copy(refs[-1].at[pl.ds(0, size - mid), cut], target.at[pl.ds(mid, size - mid)], sem).start()


def start_rest(refs, i, ends, sem, cut=slice(None), proj=None, proj_sem=None):
    ref = refs[i] if i < len(refs) - 2 else refs[-1]
    size = ends.shape[0]
    below = ref.shape[0] - size
    if proj is None:
        pltpu.make_async_copy(ref.at[pl.ds(below, size), cut], ends, sem).start()
        return
    rank, pixels = proj.shape
    packed = rank * pixels // ref.shape[1]
    below -= packed
    for n in range(rank // packed):
        part = ref.at[pl.ds(below, packed), pl.ds(n * pixels, pixels)]
        pltpu.make_async_copy(part, proj.at[pl.ds(n * packed, packed)], proj_sem).start()


def arrived(target, sem):
    pltpu.make_async_copy(target, target, sem).wait()


def row_tree_kernel(first, step, rows, rows_ref, mix_ref, *refs):
    feats = refs[:-8]
    count = len(feats) - 1
    out_ref, raw, lo, hi, ends, proj, sk, sems = refs[-8:]
    blocks, pixels, chans = raw.shape
    cols = pixels // rows
    rank = proj.shape[1]

    for i in range(count):
        j = rows_ref[i] - first + 1

        @pl.when((j >= 0) & (j < blocks))
        def fetch(i=i, j=j):
            start_map(feats, i, raw.at[j], sems.at[0, j])
            start_rest(feats, i, ends.at[j], sems.at[1, j])

        @pl.when((j >= 1) & (j < blocks - 1))
        def fetch_projector(i=i, j=j):
            start_rest(feats, i, ends.at[j], None, slice(None), proj.at[j], sems.at[2, j])

    def ready(j, wanted):
        if 0 <= first + j - 1 < count:
            arrived(raw.at[j], sems.at[0, j])
            arrived(ends.at[j], sems.at[1, j])
            side = ends[j].astype(F32)
            for h in wanted:
                shift_row(raw.at[j], lo.at[j], hi.at[j], h, cols, side)
        else:
            for h in wanted:
                for ref in (raw, lo, hi):
                    ref[j, h * cols : (h + 1) * cols] = jnp.zeros((cols, chans), BF16)

    ready(0, (rows - 1,))
    ready(1, range(rows))
    for j in range(1, blocks - 1):
        ready(j + 1, range(rows) if j + 1 < blocks - 1 else (0,))
        arrived(proj.at[j], sems.at[2, j])
        half, part = divmod(j - 1, 2)
        for a in range(3):
            for b, src in enumerate((lo, raw, hi)):
                t = 3 * a + b
                sk[half, part * rank : (part + 1) * rank, t * chans : (t + 1) * chans] = mm(
                    proj[j], rows_at(src, j, a, cols)
                ).astype(BF16)
    mix = mix_ref[...]
    left = (blocks - 2) // 2
    width = sk.shape[-1]
    starts = range(0, width, step)
    while left:
        spreads = spectral(
            [gram_terms(sk[i, :, s : s + step] for s in starts) for i in range(left)]
        )
        for i in range(left):
            mixed = combiner(mix, spreads[i])
            for s in starts:
                piece = mm(mixed, sk[i, :, s : s + step]).astype(BF16)
                if left == 1:
                    out_ref[:, s : s + step] = piece
                else:
                    sk[i // 2, (i % 2) * rank : (i % 2 + 1) * rank, s : s + step] = piece
        left //= 2


def row_tree(slots, mix, feats, first, rows, pixels):
    chans = feats[0].shape[1]
    rank = mix.shape[0]
    width = 9 * chans
    blocks = GROUP + 2
    maps = pltpu.VMEM((blocks, pixels, chans), BF16)
    return pl.pallas_call(
        functools.partial(row_tree_kernel, first, 1536, rows),
        out_shape=jax.ShapeDtypeStruct((rank, width), BF16),
        in_specs=[SMEM, VMEM] + [ANY] * len(feats),
        out_specs=VMEM,
        scratch_shapes=[
            maps,
            maps,
            maps,
            pltpu.VMEM((blocks, 4 * rows, chans), BF16),
            pltpu.VMEM((blocks, rank, pixels), BF16),
            pltpu.VMEM((GROUP // 2, 2 * rank, width), BF16),
            pltpu.SemaphoreType.DMA((3, blocks)),
        ],
        compiler_params=pltpu.CompilerParams(vmem_limit_bytes=48 << 20),
        cost_estimate=pl.CostEstimate(flops=2 * 10**10, bytes_accessed=8 << 20, transcendentals=0),
        name="row_tree",
    )(slots, mix, *placed(feats))


def own_columns(where_ref, own, others, mixed, out_ref):
    share = out_ref.shape[1]
    half = own.shape[1] // 2
    window = (share + 2 * 127) // 128 * 128
    start = where_ref[3] * share
    which = start // half
    inner = start - which * half
    base = pl.multiple_of(jnp.minimum(inner // 128 * 128, half - window), 128)
    core = where_ref[1]
    near = others[0][:, pl.ds(base, window)].astype(F32)
    far = others[1][:, pl.ds(base, window)].astype(F32)
    other = jnp.where(core == which, near, far).astype(BF16)
    part = jnp.concatenate([own[:, pl.ds(pl.multiple_of(which * half + base, 128), window)], other], axis=0)
    value = mm(mixed, part)
    value = pltpu.roll(value, (window - (inner - base)) % window, 1)
    out_ref[...] = value[:, :share].astype(BF16)


def merge_kernel(step, halves, share, where_ref, mix_ref, *refs):
    rank, width = refs[0].shape
    own = refs[0]
    others = refs[1 : 2 + halves]
    outs = refs[2 + halves :]
    if not share:
        *outs, merged, sem = outs
    half = width // 2
    core = where_ref[1]

    def spans():
        for s in range(0, width, step):
            if halves:
                which, inner = divmod(s, half)
                place = pl.multiple_of((core + which) % 2 * half + inner, 128)
                other = others[which][:, inner : inner + step]
            else:
                place, other = s, others[0][:, s : s + step]
            yield place, jnp.concatenate([own[:, pl.ds(place, step)], other], axis=0)

    spread = spectral([gram_terms(part for _, part in spans())])[0]
    if share:
        mix = mix_ref[pl.ds(pl.multiple_of(where_ref[2] * share, 16), share), :]
    else:
        mix = mix_ref[...]
    turned = jnp.concatenate([mix[:, rank:], mix[:, :rank]], axis=1)
    mix = jnp.where(where_ref[0] == 0, mix.astype(F32), turned.astype(F32)).astype(BF16)
    mixed = combiner(mix, spread)
    if share:
        own_columns(where_ref, own, others, mixed, outs[0])
        return
    for place, part in spans():
        span = pl.ds(place, step)
        merged[:, span] = mm(mixed, part).astype(BF16)
        pltpu.make_async_copy(merged.at[:, span], outs[0].at[:, span], sem).start()
    outs[1][...] = merged[:, pl.ds(pl.multiple_of(core * half, 128), half)]
    pltpu.make_async_copy(merged, outs[0], sem).wait()


def merge(where, mix, own, others, share=None):
    rank, width = own.shape
    if share:
        shapes = [jax.ShapeDtypeStruct(share, BF16)]
    else:
        shapes = [pltpu.HBM((rank, width), BF16), jax.ShapeDtypeStruct((rank, width // 2), BF16)]
    return pl.pallas_call(
        functools.partial(merge_kernel, 1152, len(others) == 2, share[0] if share else 0),
        out_shape=shapes,
        in_specs=[SMEM] + [VMEM] * (2 + len(others)),
        out_specs=[VMEM] if share else [ANY, VMEM],
        scratch_shapes=() if share else (pltpu.VMEM((rank, width), BF16), pltpu.SemaphoreType.DMA),
        compiler_params=pltpu.CompilerParams(vmem_limit_bytes=16 << 20),
        cost_estimate=pl.CostEstimate(flops=4 * 10**9, bytes_accessed=4 << 20, transcendentals=0),
        name="merge",
    )(where, mix, own, *others)


def conv_steps(rows, back, slots_ref, kernel_ref, feats, grads, out_ref, scratch):
    count = len(feats) - 1
    raw, lo, hi, ends, weights, total, sems = scratch
    pixels, chans = raw.shape[1:]
    cols = pixels // rows
    row = slots_ref[0]
    for i in range(count):
        j = slots_ref[i] - row + 1

        @pl.when((j >= 0) & (j < 3))
        def fetch(i=i, j=j):
            start_map(grads if back else feats, i, raw.at[j], sems.at[0, j])
            start_rest(feats, i, ends.at[j], sems.at[1, j])

    for t in range(9):
        pltpu.make_async_copy(
            kernel_ref.at[pl.ds(t * chans, chans)], weights.at[t], sems.at[2, t]
        ).start()
    yield

    def waits(j):
        arrived(raw.at[j], sems.at[0, j])
        arrived(ends.at[j], sems.at[1, j])

    for j, inside in ((0, row > 0), (2, row < count - 1)):

        @pl.when(jnp.logical_not(inside))
        def clear(j=j):
            raw[j] = jnp.zeros((pixels, chans), BF16)
            ends[j] = jnp.zeros(ends.shape[1:], BF16)

        pl.when(inside)(functools.partial(waits, j))
    waits(1)
    sides = [ends[j].astype(F32) for j in range(3)]
    for k in range(rows - 1, 2 * rows + 1):
        j, h = divmod(k, rows)
        shift_row(raw.at[j], lo.at[j], hi.at[j], h, cols, sides[j], int(back))
    for t in range(9):
        a, b = divmod(t, 3)
        arrived(weights.at[t], sems.at[2, t])
        if back:
            term = lax.dot_general(
                rows_at((lo, raw, hi)[2 - b], 1, 2 - a, cols),
                weights[t],
                NT,
                preferred_element_type=F32,
            )
        else:
            term = mm(rows_at((lo, raw, hi)[b], 1, a, cols), weights[t])
        total[...] = total[...] + term if t else term
    out_ref[...] = total[...].astype(BF16)


def conv_scratch(rows, pixels, chans):
    near = pltpu.VMEM((3, pixels, chans), BF16)
    return [
        near,
        near,
        near,
        pltpu.VMEM((3, 4 * rows, chans), BF16),
        pltpu.VMEM((9, chans, chans), BF16),
        pltpu.VMEM((pixels, chans), F32),
        pltpu.SemaphoreType.DMA((3, 9)),
    ]


def finish(*parts):
    for part in parts:
        next(part)
    for part in parts:
        for _ in part:
            pass


def conv_kernel(rows, back, slots_ref, kernel_ref, *refs):
    maps, out_ref, scratch = refs[:-8], refs[-8], refs[-7:]
    feats, grads = (maps[: len(maps) // 2], maps[len(maps) // 2 :]) if back else (maps, None)
    finish(conv_steps(rows, back, slots_ref, kernel_ref, feats, grads, out_ref, scratch))


def convolution(slots, kernel, feats, rows, pixels, grads=()):
    chans = kernel.shape[1]
    inputs = [kernel] + feats + list(grads)
    return pl.pallas_call(
        functools.partial(conv_kernel, rows, bool(grads)),
        out_shape=jax.ShapeDtypeStruct((pixels, chans), BF16),
        in_specs=[SMEM] + [ANY] * len(inputs),
        out_specs=VMEM,
        scratch_shapes=conv_scratch(rows, pixels, chans),
        compiler_params=pltpu.CompilerParams(vmem_limit_bytes=16 << 20),
        cost_estimate=pl.CostEstimate(flops=4 * 10**9, bytes_accessed=6 << 20, transcendentals=0),
        name="backward" if grads else "forward",
    )(slots, *placed(inputs))


def filter_steps(group, rows, where_ref, slots_ref, feats, grads, outs, scratch):
    count = len(feats) - 1
    keep_ref, give_ref = outs
    raw, lo, hi, ends, grad, total, sems = scratch
    pixels, lanes = raw.shape[1:]
    cols = pixels // rows
    pieces, taps, share, width = keep_ref.shape
    base = slots_ref[0] * share
    window = pl.multiple_of(base // lanes * lanes, lanes)
    inner = pl.multiple_of(base % lanes, 8)
    core = where_ref[1]
    cut = pl.ds(window, lanes)
    for i in range(count):
        j = slots_ref[i] + 1
        start_map(feats, i, raw.at[j], sems.at[0], cut)
        start_rest(feats, i, ends.at[j], sems.at[1], cut)
        start_map(grads, i, grad.at[j - 1], sems.at[2])
    yield
    inside = pl.ds(1, count)
    arrived(raw.at[inside], sems.at[0])
    arrived(ends.at[inside], sems.at[1])
    for j, h in ((0, rows - 1), (count + 1, 0)):
        for ref in (raw, lo, hi):
            ref[j, h * cols : (h + 1) * cols] = jnp.zeros((cols, lanes), BF16)
    for j in range(1, count + 1):
        side = ends[j].astype(F32)
        for h in range(rows):
            shift_row(raw.at[j], lo.at[j], hi.at[j], h, cols, side)
    arrived(grad, sems.at[2])
    chans = grad.shape[2]
    maps = [ref.reshape((count + 2) * pixels, lanes) for ref in (lo, raw, hi)]
    for a in range(3):
        for b, src in enumerate(maps):
            t = 3 * a + b
            for g in range(0, count, group):
                start = pixels * (g + 1) + (a - 1) * cols
                term = lax.dot_general(
                    src[start : start + group * pixels],
                    grad[g : g + group].reshape(group * pixels, chans),
                    (((0,), (0,)), ((), ())),
                    preferred_element_type=F32,
                )
                if g:
                    total[...] += term
                else:
                    total[...] = term
            mine = total[pl.ds(inner, share), :]
            for i in range(pieces):
                even = mine[:, 2 * i * width : (2 * i + 1) * width]
                odd = mine[:, (2 * i + 1) * width : (2 * i + 2) * width]
                keep_ref[i, t] = jnp.where(core == 0, even, odd)
                give_ref[i, t] = jnp.where(core == 0, odd, even).astype(BF16)


def filter_kernel(rows, where_ref, slots_ref, *refs):
    maps, outs, scratch = refs[:-9], refs[-9:-7], refs[-7:]
    feats, grads = maps[: len(maps) // 2], maps[len(maps) // 2 :]
    finish(filter_steps(GROUP, rows, where_ref, slots_ref, feats, grads, outs, scratch))


def filter_terms(where, slots, feats, grads, rows, share, col_count):
    pixels, chans = grads[0].shape
    count, lanes = len(feats) - 1, 128
    shape = (col_count // 2, 9, share, chans // col_count)
    window = pltpu.VMEM((count + 2, pixels, lanes), BF16)
    inputs = feats + grads
    return pl.pallas_call(
        functools.partial(filter_kernel, rows),
        out_shape=[jax.ShapeDtypeStruct(shape, F32), jax.ShapeDtypeStruct(shape, BF16)],
        in_specs=[SMEM, SMEM] + [ANY] * len(inputs),
        out_specs=[VMEM] * 2,
        scratch_shapes=[
            window,
            window,
            window,
            pltpu.VMEM((count + 2, 4 * rows, lanes), BF16),
            pltpu.VMEM((count, pixels, chans), BF16),
            pltpu.VMEM((lanes, chans), F32),
            pltpu.SemaphoreType.DMA((3,)),
        ],
        compiler_params=pltpu.CompilerParams(vmem_limit_bytes=(8 + count) << 20),
        cost_estimate=pl.CostEstimate(flops=5 * 10**9, bytes_accessed=4 << 20, transcendentals=0),
        name="filter_terms",
    )(where, slots, *placed(inputs))


def edge_kernel(rows, feat_ref, grad_ref, first_ref, last_ref, maps, sems):
    cols = maps.shape[1] // rows
    loads = [
        pltpu.make_async_copy(ref, maps.at[n], sems.at[n])
        for n, ref in enumerate((feat_ref, grad_ref))
    ]
    for copy in loads:
        copy.start()
    for copy in loads:
        copy.wait()
    for out, at in ((first_ref, 0), (last_ref, cols - 1)):
        cells = [
            maps[n, h * cols + at : h * cols + at + 1, :].astype(F32)
            for n in range(2)
            for h in range(rows)
        ]
        out[...] = jnp.concatenate(cells, axis=0).astype(BF16)


def edges(feat, grad, rows):
    edge = jax.ShapeDtypeStruct((2 * rows, feat.shape[1]), BF16)
    return pl.pallas_call(
        functools.partial(edge_kernel, rows),
        out_shape=[edge, edge],
        in_specs=[ANY, ANY],
        out_specs=[VMEM, VMEM],
        scratch_shapes=[pltpu.VMEM((2,) + feat.shape, BF16), pltpu.SemaphoreType.DMA((2,))],
        name="edges",
    )(*placed([feat, grad]))


def ring_row(place, count):
    return jnp.where(place < count // 2, 2 * place, 2 * (count - 1 - place) + 1)


def ring_place(row, count):
    return jnp.where(row % 2 == 0, row // 2, count - 1 - row // 2)


def after(value, *earlier):
    return lax.optimization_barrier((value,) + earlier)[0]


def body(features, kernel, out_grad, projector, mixers):
    rows, cols, chans = features.shape
    row_count, col_count = lax.axis_size("rows"), lax.axis_size("cols")
    row, col = lax.axis_index("rows"), lax.axis_index("cols")
    rank = projector.shape[0]
    levels = col_count.bit_length() - 1
    half_way, pixels = row_count // 2, rows * cols

    order = list(range(0, row_count, 2)) + list(range(row_count - 1, 0, -2))
    east = [(i, i + 1) for i in range(col_count - 1)]
    west = [(j, i) for i, j in east]
    steps = [0] + [d for s in range(1, half_way) for d in (-s, s)] + [half_way]
    place = ring_place(row, row_count)
    slots = jnp.stack([ring_row((place + d) % row_count, row_count) for d in steps]).astype(jnp.int32)
    where = jnp.stack([row, col % 2, col, row]).astype(jnp.int32)

    def send(value, d):
        hop = [(order[i], order[(i + d) % row_count]) for i in range(row_count)]
        return lax.ppermute(value, "rows", hop)

    flat, own_grad = features.reshape(pixels, chans), out_grad.reshape(pixels, chans)
    first, last = edges(flat, own_grad, rows)
    near = [lax.ppermute(last, "cols", east), lax.ppermute(first, "cols", west)]
    packed = rank * pixels // chans
    tail = [projector[n : n + packed] for n in range(0, rank, packed)]
    message = jnp.concatenate([flat, jnp.concatenate(tail, axis=1)], axis=0)
    message = jnp.pad(message, ((0, 4 * rows), (0, 0)))
    message = lax.optimization_barrier(message)
    grads = {0: own_grad}
    size = message.shape[0]
    message = lax.dynamic_update_slice(message, jnp.concatenate(near), (size - 4 * rows, 0))
    feats = {0: message}
    for s in range(1, half_way):
        for d in (1, -1):
            feats[-s * d] = send(feats[(1 - s) * d], d)
    top, bottom = feats[1 - half_way], feats[half_way - 1]
    feats[half_way] = [send(top[: size // 2], 1), send(bottom[size // 2 :], -1)]
    late_grad = after(own_grad, top, bottom)
    for d in (1, 2):
        grads[-d], grads[d] = send(late_grad, d), send(late_grad, -d)

    def listed(found, split=False):
        values = [found[d] for d in steps]
        return values[:-1] + list(values[-1]) if split else values

    feats = listed(feats, True)
    groups = [
        row_tree(slots, mixers[0], feats, start, rows, pixels)
        for start in range(0, row_count, GROUP)
    ]
    while len(groups) > 1:
        straight = where.at[0].set(0)
        groups = [
            merge(straight, mixers[0], groups[i], [groups[i + 1]])[0]
            for i in range(0, len(groups), 2)
        ]
    sketch = groups[0]

    def swap(value, level):
        return lax.ppermute(value, "cols", [(i, i ^ 1 << level) for i in range(col_count)])

    def turn(level):
        return where.at[0].set(col >> level & 1)

    swapped = swap(after(sketch, grads[1], grads[-1], grads[2], grads[-2]), 0)
    top, bottom, _ = lax.optimization_barrier((grads[-2], grads[2], sketch))
    grads[-2], grads[2] = top, bottom
    for s in range(3, half_way):
        for d in (1, -1):
            grads[-s * d] = send(grads[(1 - s) * d], d)
    split, reach = pixels // 2, half_way - 2
    grads[half_way] = [send(top[:split], reach), send(bottom[split:], -reach)]
    result = merge(turn(0), mixers[1], sketch, [swapped])
    sketch, half = result
    grads = listed(grads, True)

    share = chans // row_count
    output = convolution(after(slots, half), kernel, feats, rows, pixels)
    terms, give = filter_terms(after(where, output), slots, feats, grads, rows, share, col_count)
    grad_features = convolution(after(slots, give), kernel, feats, rows, pixels, grads)
    for level in range(levels):
        if level:
            pairs = terms.reshape((-1, 2) + terms.shape[1:])
            bit = col >> level & 1
            terms = lax.dynamic_index_in_dim(pairs, bit, 1, keepdims=False)
            give = lax.dynamic_index_in_dim(pairs, 1 - bit, 1, keepdims=False).astype(BF16)
        got = swap(give, level)
        if level < levels - 1:
            terms = terms + after(got, grad_features).astype(F32)

    for level in range(1, levels):
        mine = swap(half, level)
        if level == 1:
            mine = after(mine, grad_features)
        others = [mine, swap(mine, 0)]
        final = level == levels - 1
        share = (rank // col_count, sketch.shape[1] // row_count) if final else None
        result = merge(turn(level), mixers[1], sketch, others, share)
        sketch = result[0]
        if not final:
            half = result[1]
    grad_kernel = (terms + after(got, sketch).astype(F32))[0]
    return (
        output.reshape(features.shape),
        grad_features.reshape(features.shape),
        grad_kernel,
        sketch,
    )


def solution(mesh):
    in_specs = (P("rows", "cols", None), P(), P("rows", "cols", None), P("rows", "cols"), P())
    out_specs = (
        P("rows", "cols", None),
        P("rows", "cols", None),
        P(None, "rows", "cols"),
        P("cols", "rows"),
    )
    return jax.shard_map(body, mesh=mesh, in_specs=in_specs, out_specs=out_specs, check_vma=False)
```

```python
import functools
import jax
import jax.numpy as jnp
from jax import lax
from jax.experimental import pallas as pl
from jax.experimental.pallas import tpu as pltpu
from jax.sharding import PartitionSpec as P

NS_STEPS = 5
GROUP = 8
NT = (((1,), (1,)), ((), ()))
F32, BF16 = jnp.float32, jnp.bfloat16
VMEM = pl.BlockSpec(memory_space=pltpu.VMEM)
SMEM = pl.BlockSpec(memory_space=pltpu.SMEM)
ANY = pl.BlockSpec(memory_space=pltpu.HBM)


def mm(a, b):
    return jnp.dot(a, b, preferred_element_type=F32)


def spectral(grams):
    size = grams[0].shape[0]
    rows = lax.broadcasted_iota(jnp.int32, (size, size), 0)
    cols = lax.broadcasted_iota(jnp.int32, (size, size), 1)
    diagonal = rows == cols

    def total(x):
        return jnp.sum(jnp.sum(x, axis=1, keepdims=True), axis=0, keepdims=True)

    spreads = []
    for gram in grams:
        trace = total(jnp.where(diagonal, gram, 0.0))
        spread = gram / (trace + 1e-06) - jnp.where(diagonal, 1.0 / size, 0.0)
        spreads.append(spread / (jnp.sqrt(total(spread * spread)) + 1e-06))
    for sweep in range(NS_STEPS - 1):
        low = [y.astype(BF16) for y in spreads]
        squares = [mm(y, y).astype(BF16) for y in low]
        spreads = [1.5 * s - 0.5 * mm(y, z) for s, y, z in zip(spreads, low, squares)]
    return spreads


def combiner(mix, spread):
    low = spread.astype(BF16)
    square = mm(low, low).astype(BF16)
    once = mm(mix, low)
    turned = 1.5 * once - 0.5 * mm(once.astype(BF16), square)
    return (0.5 * (mix.astype(F32) + turned)).astype(BF16)


def gram_terms(parts):
    total = None
    for part in parts:
        term = lax.dot_general(part, part, NT, preferred_element_type=F32)
        total = term if total is None else total + term
    return total


def shifted(block, left, right):
    at = lax.broadcasted_iota(jnp.int32, block.shape, 0)
    wide = block.astype(F32)
    size = block.shape[0]
    low = jnp.where(at == 0, left, pltpu.roll(wide, 1, 0)).astype(BF16)
    high = jnp.where(at == size - 1, right, pltpu.roll(wide, size - 1, 0)).astype(BF16)
    return low, high


def rows_at(src, j, a, cols):
    size = src.shape[1]
    if a == 1:
        return src[j]
    if a == 0:
        return jnp.concatenate([src[j - 1, size - cols : size], src[j, : size - cols]], axis=0)
    return jnp.concatenate([src[j, cols:size], src[j + 1, :cols]], axis=0)


def shift_row(raw, lo, hi, h, cols, side):
    rows = side.shape[0] // 2
    at = slice(h * cols, (h + 1) * cols)
    lo[at], hi[at] = shifted(raw[at], side[h : h + 1], side[rows + h : rows + h + 1])


def placed(values):
    return [pltpu.with_memory_space_constraint(x, pltpu.HBM) for x in values]


def start_map(refs, i, target, sem, cut=slice(None)):
    size = target.shape[0]
    if i < len(refs) - 2:
        pltpu.make_async_copy(refs[i].at[pl.ds(0, size), cut], target, sem).start()
    else:
        mid = refs[-2].shape[0]
        pltpu.make_async_copy(refs[-2].at[:, cut], target.at[pl.ds(0, mid)], sem).start()
        pltpu.make_async_copy(refs[-1].at[pl.ds(0, size - mid), cut], target.at[pl.ds(mid, size - mid)], sem).start()


def start_rest(refs, i, ends, sem, cut=slice(None), proj=None, proj_sem=None):
    ref = refs[i] if i < len(refs) - 2 else refs[-1]
    size = ends.shape[0]
    below = ref.shape[0] - size
    if proj is None:
        pltpu.make_async_copy(ref.at[pl.ds(below, size), cut], ends, sem).start()
        return
    rank, pixels = proj.shape
    packed = rank * pixels // ref.shape[1]
    below -= packed
    for n in range(rank // packed):
        part = ref.at[pl.ds(below, packed), pl.ds(n * pixels, pixels)]
        pltpu.make_async_copy(part, proj.at[pl.ds(n * packed, packed)], proj_sem).start()


def arrived(target, sem):
    pltpu.make_async_copy(target, target, sem).wait()


def row_tree_kernel(first, step, rows, rows_ref, mix_ref, *refs):
    feats = refs[:-8]
    count = len(feats) - 1
    out_ref, raw, lo, hi, ends, proj, sk, sems = refs[-8:]
    blocks, pixels, chans = raw.shape
    cols = pixels // rows
    rank = proj.shape[1]

    for i in range(count):
        j = rows_ref[i] - first + 1

        @pl.when((j >= 0) & (j < blocks))
        def fetch(i=i, j=j):
            start_map(feats, i, raw.at[j], sems.at[0, j])
            start_rest(feats, i, ends.at[j], sems.at[1, j])

        @pl.when((j >= 1) & (j < blocks - 1))
        def fetch_projector(i=i, j=j):
            start_rest(feats, i, ends.at[j], None, slice(None), proj.at[j], sems.at[2, j])

    def ready(j, wanted):
        if 0 <= first + j - 1 < count:
            arrived(raw.at[j], sems.at[0, j])
            arrived(ends.at[j], sems.at[1, j])
            side = ends[j].astype(F32)
            for h in wanted:
                shift_row(raw.at[j], lo.at[j], hi.at[j], h, cols, side)
        else:
            for h in wanted:
                for ref in (raw, lo, hi):
                    ref[j, h * cols : (h + 1) * cols] = jnp.zeros((cols, chans), BF16)

    ready(0, (rows - 1,))
    ready(1, range(rows))
    for j in range(1, blocks - 1):
        ready(j + 1, range(rows) if j + 1 < blocks - 1 else (0,))
        arrived(proj.at[j], sems.at[2, j])
        half, part = divmod(j - 1, 2)
        for a in range(3):
            for b, src in enumerate((lo, raw, hi)):
                t = 3 * a + b
                sk[half, part * rank : (part + 1) * rank, t * chans : (t + 1) * chans] = mm(
                    proj[j], rows_at(src, j, a, cols)
                ).astype(BF16)
    mix = mix_ref[...]
    left = (blocks - 2) // 2
    width = sk.shape[-1]
    starts = range(0, width, step)
    while left:
        spreads = spectral(
            [gram_terms(sk[i, :, s : s + step] for s in starts) for i in range(left)]
        )
        for i in range(left):
            mixed = combiner(mix, spreads[i])
            for s in starts:
                piece = mm(mixed, sk[i, :, s : s + step]).astype(BF16)
                if left == 1:
                    out_ref[:, s : s + step] = piece
                else:
                    sk[i // 2, (i % 2) * rank : (i % 2 + 1) * rank, s : s + step] = piece
        left //= 2


def row_tree(slots, mix, feats, first, rows, pixels):
    chans = feats[0].shape[1]
    rank = mix.shape[0]
    width = 9 * chans
    blocks = GROUP + 2
    maps = pltpu.VMEM((blocks, pixels, chans), BF16)
    return pl.pallas_call(
        functools.partial(row_tree_kernel, first, 1536, rows),
        out_shape=jax.ShapeDtypeStruct((rank, width), BF16),
        in_specs=[SMEM, VMEM] + [ANY] * len(feats),
        out_specs=VMEM,
        scratch_shapes=[
            maps,
            maps,
            maps,
            pltpu.VMEM((blocks, 2 * rows, chans), BF16),
            pltpu.VMEM((blocks, rank, pixels), BF16),
            pltpu.VMEM((GROUP // 2, 2 * rank, width), BF16),
            pltpu.SemaphoreType.DMA((3, blocks)),
        ],
        compiler_params=pltpu.CompilerParams(vmem_limit_bytes=48 << 20),
        cost_estimate=pl.CostEstimate(flops=2 * 10**10, bytes_accessed=8 << 20, transcendentals=0),
        name="row_tree",
    )(slots, mix, *placed(feats))


def own_columns(where_ref, own, others, mixed, out_ref):
    share = out_ref.shape[1]
    half = own.shape[1] // 2
    window = (share + 2 * 127) // 128 * 128
    start = where_ref[3] * share
    which = start // half
    inner = start - which * half
    base = pl.multiple_of(jnp.minimum(inner // 128 * 128, half - window), 128)
    core = where_ref[1]
    near = others[0][:, pl.ds(base, window)].astype(F32)
    far = others[1][:, pl.ds(base, window)].astype(F32)
    other = jnp.where(core == which, near, far).astype(BF16)
    part = jnp.concatenate([own[:, pl.ds(pl.multiple_of(which * half + base, 128), window)], other], axis=0)
    value = mm(mixed, part)
    value = pltpu.roll(value, (window - (inner - base)) % window, 1)
    out_ref[...] = value[:, :share].astype(BF16)


def merge_kernel(step, halves, share, where_ref, mix_ref, *refs):
    rank, width = refs[0].shape
    own = refs[0]
    others = refs[1 : 2 + halves]
    outs = refs[2 + halves :]
    if not share:
        *outs, merged, sem = outs
    half = width // 2
    core = where_ref[1]

    def spans():
        for s in range(0, width, step):
            if halves:
                which, inner = divmod(s, half)
                place = pl.multiple_of((core + which) % 2 * half + inner, 128)
                other = others[which][:, inner : inner + step]
            else:
                place, other = s, others[0][:, s : s + step]
            yield place, jnp.concatenate([own[:, pl.ds(place, step)], other], axis=0)

    spread = spectral([gram_terms(part for _, part in spans())])[0]
    if share:
        mix = mix_ref[pl.ds(pl.multiple_of(where_ref[2] * share, 16), share), :]
    else:
        mix = mix_ref[...]
    turned = jnp.concatenate([mix[:, rank:], mix[:, :rank]], axis=1)
    mix = jnp.where(where_ref[0] == 0, mix.astype(F32), turned.astype(F32)).astype(BF16)
    mixed = combiner(mix, spread)
    if share:
        own_columns(where_ref, own, others, mixed, outs[0])
        return
    for place, part in spans():
        span = pl.ds(place, step)
        merged[:, span] = mm(mixed, part).astype(BF16)
        pltpu.make_async_copy(merged.at[:, span], outs[0].at[:, span], sem).start()
    outs[1][...] = merged[:, pl.ds(pl.multiple_of(core * half, 128), half)]
    pltpu.make_async_copy(merged, outs[0], sem).wait()


def merge(where, mix, own, others, share=None):
    rank, width = own.shape
    if share:
        shapes = [jax.ShapeDtypeStruct(share, BF16)]
    else:
        shapes = [pltpu.HBM((rank, width), BF16), jax.ShapeDtypeStruct((rank, width // 2), BF16)]
    return pl.pallas_call(
        functools.partial(merge_kernel, 1152, len(others) == 2, share[0] if share else 0),
        out_shape=shapes,
        in_specs=[SMEM] + [VMEM] * (2 + len(others)),
        out_specs=[VMEM] if share else [ANY, VMEM],
        scratch_shapes=() if share else (pltpu.VMEM((rank, width), BF16), pltpu.SemaphoreType.DMA),
        compiler_params=pltpu.CompilerParams(vmem_limit_bytes=16 << 20),
        cost_estimate=pl.CostEstimate(flops=4 * 10**9, bytes_accessed=4 << 20, transcendentals=0),
        name="merge",
    )(where, mix, own, *others)


def start_weights(kernel_ref, weights, sems):
    chans = weights.shape[1]
    for t in range(9):
        pltpu.make_async_copy(
            kernel_ref.at[pl.ds(t * chans, chans)], weights.at[t], sems.at[t]
        ).start()


def tap_sums(patch, weights, sems, totals):
    for t in range(9):
        arrived(weights.at[t], sems.at[t])
        terms = [
            mm(patch(0, t // 3, t % 3), weights[t]),
            lax.dot_general(
                patch(1, 2 - t // 3, 2 - t % 3), weights[t], NT, preferred_element_type=F32
            ),
        ]
        for n, term in enumerate(terms):
            totals[n] = totals[n] + term if t else term


def conv_kernel(rows, kernel_ref, feat_ref, grad_ref, above_ref, below_ref, west_ref, east_ref, out_ref, back_ref, raw, lo, hi, sides, weights, totals, sems):
    pixels, chans = feat_ref.shape
    cols = pixels // rows
    loads = [
        (feat_ref, raw.at[0, pl.ds(cols, pixels)]),
        (grad_ref, raw.at[1, pl.ds(cols, pixels)]),
        (west_ref, sides.at[0]),
        (east_ref, sides.at[1]),
    ]
    for k, ref in enumerate((above_ref, below_ref)):
        for n in range(2):
            part = raw.at[n, pl.ds(k * (cols + pixels), cols)]
            loads.append((ref.at[pl.ds(n * cols, cols)], part))
        loads.append((ref.at[pl.ds(2 * cols, 2 * rows)], sides.at[2 + k]))
    loads = [pltpu.make_async_copy(*load, sems.at[9 + n]) for n, load in enumerate(loads)]
    for copy in loads:
        copy.start()
    start_weights(kernel_ref, weights, sems)
    for copy in loads:
        copy.wait()
    west, east, above, below = [sides[n].astype(F32) for n in range(4)]
    for n in range(2):
        mine = slice(n * rows, (n + 1) * rows)
        corner = [2 * n, 2 * n + 1]
        side = jnp.concatenate(
            [
                piece
                for k, cells in zip(corner, (west, east))
                for piece in (above[k : k + 1], cells[mine], below[k : k + 1])
            ],
            axis=0,
        )
        for h in range(rows + 2):
            shift_row(raw.at[n], lo.at[n], hi.at[n], h, cols, side)

    def patch(n, a, b):
        return (lo, raw, hi)[b][n, a * cols : a * cols + pixels]

    tap_sums(patch, weights, sems, totals)
    for n, ref in enumerate((out_ref, back_ref)):
        ref[...] = totals[n].astype(BF16)


def convolutions(kernel, feat, grad, beyond, near, rows):
    pixels, chans = feat.shape
    cols = pixels // rows
    block = jax.ShapeDtypeStruct((pixels, chans), BF16)
    maps = pltpu.VMEM((2, pixels + 2 * cols, chans), BF16)
    return pl.pallas_call(
        functools.partial(conv_kernel, rows),
        out_shape=[block, block],
        in_specs=[ANY] * 7,
        out_specs=[VMEM, VMEM],
        scratch_shapes=[
            maps,
            maps,
            maps,
            pltpu.VMEM((4, 2 * rows, chans), BF16),
            pltpu.VMEM((9, chans, chans), BF16),
            pltpu.VMEM((2, pixels, chans), F32),
            pltpu.SemaphoreType.DMA((19,)),
        ],
        compiler_params=pltpu.CompilerParams(vmem_limit_bytes=16 << 20),
        cost_estimate=pl.CostEstimate(flops=6 * 10**9, bytes_accessed=6 << 20, transcendentals=0),
        name="convolutions",
    )(*placed([kernel, feat, grad] + beyond + near))


def filter_kernel(group, rows, where_ref, slots_ref, *refs):
    maps, refs = refs[:-9], refs[-9:]
    feats, grads = maps[: len(maps) // 2], maps[len(maps) // 2 :]
    count = len(feats) - 1
    keep_ref, give_ref, raw, lo, hi, ends, grad, total, sems = refs
    pixels, lanes = raw.shape[1:]
    cols = pixels // rows
    pieces, taps, share, width = keep_ref.shape
    base = slots_ref[0] * share
    window = pl.multiple_of(base // lanes * lanes, lanes)
    inner = pl.multiple_of(base % lanes, 8)
    core = where_ref[1]
    cut = pl.ds(window, lanes)
    for i in range(count):
        j = slots_ref[i] + 1
        start_map(feats, i, raw.at[j], sems.at[0], cut)
        start_rest(feats, i, ends.at[j], sems.at[1], cut)
        start_map(grads, i, grad.at[j - 1], sems.at[2])
    inside = pl.ds(1, count)
    arrived(raw.at[inside], sems.at[0])
    arrived(ends.at[inside], sems.at[1])
    for j, h in ((0, rows - 1), (count + 1, 0)):
        for ref in (raw, lo, hi):
            ref[j, h * cols : (h + 1) * cols] = jnp.zeros((cols, lanes), BF16)
    for j in range(1, count + 1):
        side = ends[j].astype(F32)
        for h in range(rows):
            shift_row(raw.at[j], lo.at[j], hi.at[j], h, cols, side)
    arrived(grad, sems.at[2])
    chans = grad.shape[2]
    maps = [ref.reshape((count + 2) * pixels, lanes) for ref in (lo, raw, hi)]
    for a in range(3):
        for b, src in enumerate(maps):
            t = 3 * a + b
            for g in range(0, count, group):
                start = pixels * (g + 1) + (a - 1) * cols
                term = lax.dot_general(
                    src[start : start + group * pixels],
                    grad[g : g + group].reshape(group * pixels, chans),
                    (((0,), (0,)), ((), ())),
                    preferred_element_type=F32,
                )
                if g:
                    total[...] += term
                else:
                    total[...] = term
            mine = total[pl.ds(inner, share), :]
            for i in range(pieces):
                even = mine[:, 2 * i * width : (2 * i + 1) * width]
                odd = mine[:, (2 * i + 1) * width : (2 * i + 2) * width]
                keep_ref[i, t] = jnp.where(core == 0, even, odd)
                give_ref[i, t] = jnp.where(core == 0, odd, even).astype(BF16)


def filter_terms(where, slots, feats, grads, rows, share, col_count):
    pixels, chans = grads[0].shape
    count, lanes = len(feats) - 1, 128
    shape = (col_count // 2, 9, share, chans // col_count)
    window = pltpu.VMEM((count + 2, pixels, lanes), BF16)
    inputs = feats + grads
    return pl.pallas_call(
        functools.partial(filter_kernel, GROUP, rows),
        out_shape=[jax.ShapeDtypeStruct(shape, F32), jax.ShapeDtypeStruct(shape, BF16)],
        in_specs=[SMEM, SMEM] + [ANY] * len(inputs),
        out_specs=[VMEM] * 2,
        scratch_shapes=[
            window,
            window,
            window,
            pltpu.VMEM((count + 2, 2 * rows, lanes), BF16),
            pltpu.VMEM((count, pixels, chans), BF16),
            pltpu.VMEM((lanes, chans), F32),
            pltpu.SemaphoreType.DMA((3,)),
        ],
        compiler_params=pltpu.CompilerParams(vmem_limit_bytes=(8 + count) << 20),
        cost_estimate=pl.CostEstimate(flops=5 * 10**9, bytes_accessed=4 << 20, transcendentals=0),
        name="filter_terms",
    )(where, slots, *placed(inputs))


def edge_kernel(rows, feat_ref, grad_ref, first_ref, last_ref, maps, sems):
    cols = maps.shape[1] // rows
    loads = [
        pltpu.make_async_copy(ref, maps.at[n], sems.at[n])
        for n, ref in enumerate((feat_ref, grad_ref))
    ]
    for copy in loads:
        copy.start()
    for copy in loads:
        copy.wait()
    for out, at in ((first_ref, 0), (last_ref, cols - 1)):
        cells = [
            maps[n, h * cols + at : h * cols + at + 1, :].astype(F32)
            for n in range(2)
            for h in range(rows)
        ]
        out[...] = jnp.concatenate(cells, axis=0).astype(BF16)


def edges(feat, grad, rows):
    edge = jax.ShapeDtypeStruct((2 * rows, feat.shape[1]), BF16)
    return pl.pallas_call(
        functools.partial(edge_kernel, rows),
        out_shape=[edge, edge],
        in_specs=[ANY, ANY],
        out_specs=[VMEM, VMEM],
        scratch_shapes=[pltpu.VMEM((2,) + feat.shape, BF16), pltpu.SemaphoreType.DMA((2,))],
        name="edges",
    )(*placed([feat, grad]))


def ring_row(place, count):
    return jnp.where(place < count // 2, 2 * place, 2 * (count - 1 - place) + 1)


def ring_place(row, count):
    return jnp.where(row % 2 == 0, row // 2, count - 1 - row // 2)


def after(value, *earlier):
    return lax.optimization_barrier((value,) + earlier)[0]


def body(features, kernel, out_grad, projector, mixers):
    rows, cols, chans = features.shape
    row_count, col_count = lax.axis_size("rows"), lax.axis_size("cols")
    row, col = lax.axis_index("rows"), lax.axis_index("cols")
    rank = projector.shape[0]
    levels = col_count.bit_length() - 1
    half_way, pixels = row_count // 2, rows * cols

    order = list(range(0, row_count, 2)) + list(range(row_count - 1, 0, -2))
    east = [(i, i + 1) for i in range(col_count - 1)]
    west = [(j, i) for i, j in east]
    steps = [0] + [d for s in range(1, half_way) for d in (-s, s)] + [half_way]
    place = ring_place(row, row_count)
    slots = jnp.stack([ring_row((place + d) % row_count, row_count) for d in steps]).astype(jnp.int32)
    where = jnp.stack([row, col % 2, col, row]).astype(jnp.int32)

    def send(value, d):
        hop = [(order[i], order[(i + d) % row_count]) for i in range(row_count)]
        return lax.ppermute(value, "rows", hop)

    flat, own_grad = features.reshape(pixels, chans), out_grad.reshape(pixels, chans)
    first, last = edges(flat, own_grad, rows)
    near = [lax.ppermute(last, "cols", east), lax.ppermute(first, "cols", west)]
    packed = rank * pixels // chans
    tail = [projector[n : n + packed] for n in range(0, rank, packed)]
    message = jnp.concatenate([flat, jnp.concatenate(tail, axis=1)], axis=0)
    message = jnp.pad(message, ((0, 2 * rows), (0, 0)))
    message = lax.optimization_barrier(message)
    size = message.shape[0]
    sides = jnp.concatenate([x[:rows] for x in near])
    message = lax.dynamic_update_slice(message, sides, (size - 2 * rows, 0))
    feats = {0: message}
    beyond = []
    south = [(i, i + 1) for i in range(row_count - 1)]
    north = [(j, i) for i, j in south]
    for h, perm in ((rows - 1, south), (0, north)):
        cells = [x[n * rows + h : n * rows + h + 1] for n in range(2) for x in near]
        row_of = [x[h * cols : (h + 1) * cols] for x in (flat, own_grad)]
        parcel = jnp.concatenate(row_of + cells)
        parcel = jnp.pad(parcel, ((0, 2 * rows - len(cells)), (0, 0)))
        beyond.append(lax.ppermute(parcel, "rows", perm))
    for s in range(1, half_way):
        for d in (1, -1):
            feats[-s * d] = send(feats[(1 - s) * d], d)
    output, grad_features = convolutions(kernel, flat, own_grad, beyond, near, rows)
    feats[1 - half_way], feats[half_way - 1], output, grad_features = lax.optimization_barrier(
        (feats[1 - half_way], feats[half_way - 1], output, grad_features)
    )
    top, bottom = feats[1 - half_way], feats[half_way - 1]
    mid = size // 32 * 16
    feats[half_way] = [send(top[:mid], 1), send(bottom[mid:], -1)]
    grads = {0: own_grad}
    late_grad = after(own_grad, top, bottom)
    for d in (1, 2):
        grads[-d], grads[d] = send(late_grad, d), send(late_grad, -d)

    def listed(found, split=False):
        values = [found[d] for d in steps]
        return values[:-1] + list(values[-1]) if split else values

    feats = listed(feats, True)
    groups = [
        row_tree(slots, mixers[0], feats, start, rows, pixels)
        for start in range(0, row_count, GROUP)
    ]
    while len(groups) > 1:
        straight = where.at[0].set(0)
        groups = [
            merge(straight, mixers[0], groups[i], [groups[i + 1]])[0]
            for i in range(0, len(groups), 2)
        ]
    sketch = groups[0]

    def swap(value, level):
        return lax.ppermute(value, "cols", [(i, i ^ 1 << level) for i in range(col_count)])

    def turn(level):
        return where.at[0].set(col >> level & 1)

    swapped = swap(after(sketch, grads[1], grads[-1], grads[2], grads[-2]), 0)
    top, bottom, _ = lax.optimization_barrier((grads[-2], grads[2], sketch))
    grads[-2], grads[2] = top, bottom
    for s in range(3, half_way):
        for d in (1, -1):
            grads[-s * d] = send(grads[(1 - s) * d], d)
    split, reach = pixels // 2, half_way - 2
    grads[half_way] = [send(top[:split], reach), send(bottom[split:], -reach)]
    result = merge(turn(0), mixers[1], sketch, [swapped])
    sketch, half = result
    grads = listed(grads, True)

    share = chans // row_count
    terms, give = filter_terms(after(where, half), slots, feats, grads, rows, share, col_count)
    filtered = give
    for level in range(levels):
        if level:
            pairs = terms.reshape((-1, 2) + terms.shape[1:])
            bit = col >> level & 1
            terms = lax.dynamic_index_in_dim(pairs, bit, 1, keepdims=False)
            give = lax.dynamic_index_in_dim(pairs, 1 - bit, 1, keepdims=False).astype(BF16)
        got = swap(give, level)
        if level < levels - 1:
            terms = terms + got.astype(F32)

    for level in range(1, levels):
        mine = swap(half, level)
        if level == 1:
            mine = after(mine, filtered)
        others = [mine, swap(mine, 0)]
        final = level == levels - 1
        share = (rank // col_count, sketch.shape[1] // row_count) if final else None
        result = merge(turn(level), mixers[1], sketch, others, share)
        sketch = result[0]
        if not final:
            half = result[1]
    grad_kernel = (terms + after(got, sketch).astype(F32))[0]
    return (
        output.reshape(features.shape),
        grad_features.reshape(features.shape),
        grad_kernel,
        sketch,
    )


def solution(mesh):
    in_specs = (P("rows", "cols", None), P(), P("rows", "cols", None), P("rows", "cols"), P())
    out_specs = (
        P("rows", "cols", None),
        P("rows", "cols", None),
        P(None, "rows", "cols"),
        P("cols", "rows"),
    )
    return jax.shard_map(body, mesh=mesh, in_specs=in_specs, out_specs=out_specs, check_vma=False)
```

```python
import functools
import jax
import jax.numpy as jnp
from jax import lax
from jax.experimental import pallas as pl
from jax.experimental.pallas import tpu as pltpu
from jax.sharding import PartitionSpec as P

NS_STEPS = 5
GROUP = 8
NT = (((1,), (1,)), ((), ()))
F32, BF16 = jnp.float32, jnp.bfloat16
VMEM = pl.BlockSpec(memory_space=pltpu.VMEM)
SMEM = pl.BlockSpec(memory_space=pltpu.SMEM)
ANY = pl.BlockSpec(memory_space=pltpu.HBM)


def mm(a, b):
    return jnp.dot(a, b, preferred_element_type=F32)


def spectral(grams):
    size = grams[0].shape[0]
    rows = lax.broadcasted_iota(jnp.int32, (size, size), 0)
    cols = lax.broadcasted_iota(jnp.int32, (size, size), 1)
    diagonal = rows == cols

    def total(x):
        return jnp.sum(jnp.sum(x, axis=1, keepdims=True), axis=0, keepdims=True)

    spreads = []
    for gram in grams:
        trace = total(jnp.where(diagonal, gram, 0.0))
        spread = gram / (trace + 1e-06) - jnp.where(diagonal, 1.0 / size, 0.0)
        spreads.append(spread / (jnp.sqrt(total(spread * spread)) + 1e-06))
    for sweep in range(NS_STEPS - 1):
        low = [y.astype(BF16) for y in spreads]
        squares = [mm(y, y).astype(BF16) for y in low]
        spreads = [1.5 * s - 0.5 * mm(y, z) for s, y, z in zip(spreads, low, squares)]
    return spreads


def combiner(mix, spread):
    low = spread.astype(BF16)
    square = mm(low, low).astype(BF16)
    once = mm(mix, low)
    turned = 1.5 * once - 0.5 * mm(once.astype(BF16), square)
    return (0.5 * (mix.astype(F32) + turned)).astype(BF16)


def gram_terms(parts):
    total = None
    for part in parts:
        term = lax.dot_general(part, part, NT, preferred_element_type=F32)
        total = term if total is None else total + term
    return total


def shifted(block, left, right):
    at = lax.broadcasted_iota(jnp.int32, block.shape, 0)
    wide = block.astype(F32)
    size = block.shape[0]
    low = jnp.where(at == 0, left, pltpu.roll(wide, 1, 0)).astype(BF16)
    high = jnp.where(at == size - 1, right, pltpu.roll(wide, size - 1, 0)).astype(BF16)
    return low, high


def rows_at(src, j, a, cols):
    size = src.shape[1]
    if a == 1:
        return src[j]
    if a == 0:
        return jnp.concatenate([src[j - 1, size - cols : size], src[j, : size - cols]], axis=0)
    return jnp.concatenate([src[j, cols:size], src[j + 1, :cols]], axis=0)


def shift_row(raw, lo, hi, h, cols, side):
    rows = side.shape[0] // 2
    at = slice(h * cols, (h + 1) * cols)
    lo[at], hi[at] = shifted(raw[at], side[h : h + 1], side[rows + h : rows + h + 1])


def placed(values):
    return [pltpu.with_memory_space_constraint(x, pltpu.HBM) for x in values]


def start_map(refs, i, target, sem, cut=slice(None)):
    size = target.shape[0]
    if i < len(refs) - 2:
        pltpu.make_async_copy(refs[i].at[pl.ds(0, size), cut], target, sem).start()
    else:
        mid = refs[-2].shape[0]
        pltpu.make_async_copy(refs[-2].at[:, cut], target.at[pl.ds(0, mid)], sem).start()
        pltpu.make_async_copy(refs[-1].at[pl.ds(0, size - mid), cut], target.at[pl.ds(mid, size - mid)], sem).start()


def start_rest(refs, i, ends, sem, cut=slice(None), proj=None, proj_sem=None):
    ref = refs[i] if i < len(refs) - 2 else refs[-1]
    size = ends.shape[0]
    below = ref.shape[0] - size
    if proj is None:
        pltpu.make_async_copy(ref.at[pl.ds(below, size), cut], ends, sem).start()
        return
    rank, pixels = proj.shape
    packed = rank * pixels // ref.shape[1]
    below -= packed
    for n in range(rank // packed):
        part = ref.at[pl.ds(below, packed), pl.ds(n * pixels, pixels)]
        pltpu.make_async_copy(part, proj.at[pl.ds(n * packed, packed)], proj_sem).start()


def arrived(target, sem):
    pltpu.make_async_copy(target, target, sem).wait()


def row_tree_kernel(first, step, rows, rows_ref, mix_ref, *refs):
    feats = refs[:-8]
    count = len(feats) - 1
    out_ref, raw, lo, hi, ends, proj, sk, sems = refs[-8:]
    blocks, pixels, chans = raw.shape
    cols = pixels // rows
    rank = proj.shape[1]

    for i in range(count):
        j = rows_ref[i] - first + 1

        @pl.when((j >= 0) & (j < blocks))
        def fetch(i=i, j=j):
            start_map(feats, i, raw.at[j], sems.at[0, j])
            start_rest(feats, i, ends.at[j], sems.at[1, j])

        @pl.when((j >= 1) & (j < blocks - 1))
        def fetch_projector(i=i, j=j):
            start_rest(feats, i, ends.at[j], None, slice(None), proj.at[j], sems.at[2, j])

    def ready(j, wanted):
        if 0 <= first + j - 1 < count:
            arrived(raw.at[j], sems.at[0, j])
            arrived(ends.at[j], sems.at[1, j])
            side = ends[j].astype(F32)
            for h in wanted:
                shift_row(raw.at[j], lo.at[j], hi.at[j], h, cols, side)
        else:
            for h in wanted:
                for ref in (raw, lo, hi):
                    ref[j, h * cols : (h + 1) * cols] = jnp.zeros((cols, chans), BF16)

    ready(0, (rows - 1,))
    ready(1, range(rows))
    for j in range(1, blocks - 1):
        ready(j + 1, range(rows) if j + 1 < blocks - 1 else (0,))
        arrived(proj.at[j], sems.at[2, j])
        half, part = divmod(j - 1, 2)
        for a in range(3):
            for b, src in enumerate((lo, raw, hi)):
                t = 3 * a + b
                sk[half, part * rank : (part + 1) * rank, t * chans : (t + 1) * chans] = mm(
                    proj[j], rows_at(src, j, a, cols)
                ).astype(BF16)
    mix = mix_ref[...]
    left = (blocks - 2) // 2
    width = sk.shape[-1]
    starts = range(0, width, step)
    while left:
        spreads = spectral(
            [gram_terms(sk[i, :, s : s + step] for s in starts) for i in range(left)]
        )
        for i in range(left):
            mixed = combiner(mix, spreads[i])
            for s in starts:
                piece = mm(mixed, sk[i, :, s : s + step]).astype(BF16)
                if left == 1:
                    out_ref[:, s : s + step] = piece
                else:
                    sk[i // 2, (i % 2) * rank : (i % 2 + 1) * rank, s : s + step] = piece
        left //= 2


def row_tree(slots, mix, feats, first, rows, pixels):
    chans = feats[0].shape[1]
    rank = mix.shape[0]
    width = 9 * chans
    blocks = GROUP + 2
    maps = pltpu.VMEM((blocks, pixels, chans), BF16)
    return pl.pallas_call(
        functools.partial(row_tree_kernel, first, 1536, rows),
        out_shape=jax.ShapeDtypeStruct((rank, width), BF16),
        in_specs=[SMEM, VMEM] + [ANY] * len(feats),
        out_specs=VMEM,
        scratch_shapes=[
            maps,
            maps,
            maps,
            pltpu.VMEM((blocks, 2 * rows, chans), BF16),
            pltpu.VMEM((blocks, rank, pixels), BF16),
            pltpu.VMEM((GROUP // 2, 2 * rank, width), BF16),
            pltpu.SemaphoreType.DMA((3, blocks)),
        ],
        compiler_params=pltpu.CompilerParams(vmem_limit_bytes=48 << 20),
        cost_estimate=pl.CostEstimate(flops=2 * 10**10, bytes_accessed=8 << 20, transcendentals=0),
        name="row_tree",
    )(slots, mix, *placed(feats))


def own_columns(where_ref, own, others, mixed, out_ref):
    share = out_ref.shape[1]
    half = own.shape[1] // 2
    window = (share + 2 * 127) // 128 * 128
    start = where_ref[3] * share
    which = start // half
    inner = start - which * half
    base = pl.multiple_of(jnp.minimum(inner // 128 * 128, half - window), 128)
    core = where_ref[1]
    near = others[0][:, pl.ds(base, window)].astype(F32)
    far = others[1][:, pl.ds(base, window)].astype(F32)
    other = jnp.where(core == which, near, far).astype(BF16)
    part = jnp.concatenate([own[:, pl.ds(pl.multiple_of(which * half + base, 128), window)], other], axis=0)
    value = mm(mixed, part)
    value = pltpu.roll(value, (window - (inner - base)) % window, 1)
    out_ref[...] = value[:, :share].astype(BF16)


def merge_kernel(step, halves, share, where_ref, mix_ref, *refs):
    rank, width = refs[0].shape
    own = refs[0]
    others = refs[1 : 2 + halves]
    outs = refs[2 + halves :]
    if not share:
        *outs, merged, sem = outs
    half = width // 2
    core = where_ref[1]

    def spans():
        for s in range(0, width, step):
            if halves:
                which, inner = divmod(s, half)
                place = pl.multiple_of((core + which) % 2 * half + inner, 128)
                other = others[which][:, inner : inner + step]
            else:
                place, other = s, others[0][:, s : s + step]
            yield place, jnp.concatenate([own[:, pl.ds(place, step)], other], axis=0)

    spread = spectral([gram_terms(part for _, part in spans())])[0]
    if share:
        mix = mix_ref[pl.ds(pl.multiple_of(where_ref[2] * share, 16), share), :]
    else:
        mix = mix_ref[...]
    turned = jnp.concatenate([mix[:, rank:], mix[:, :rank]], axis=1)
    mix = jnp.where(where_ref[0] == 0, mix.astype(F32), turned.astype(F32)).astype(BF16)
    mixed = combiner(mix, spread)
    if share:
        own_columns(where_ref, own, others, mixed, outs[0])
        return
    for place, part in spans():
        span = pl.ds(place, step)
        merged[:, span] = mm(mixed, part).astype(BF16)
        pltpu.make_async_copy(merged.at[:, span], outs[0].at[:, span], sem).start()
    outs[1][...] = merged[:, pl.ds(pl.multiple_of(core * half, 128), half)]
    pltpu.make_async_copy(merged, outs[0], sem).wait()


def merge(where, mix, own, others, share=None):
    rank, width = own.shape
    if share:
        shapes = [jax.ShapeDtypeStruct(share, BF16)]
    else:
        shapes = [pltpu.HBM((rank, width), BF16), jax.ShapeDtypeStruct((rank, width // 2), BF16)]
    return pl.pallas_call(
        functools.partial(merge_kernel, 1152, len(others) == 2, share[0] if share else 0),
        out_shape=shapes,
        in_specs=[SMEM] + [VMEM] * (2 + len(others)),
        out_specs=[VMEM] if share else [ANY, VMEM],
        scratch_shapes=() if share else (pltpu.VMEM((rank, width), BF16), pltpu.SemaphoreType.DMA),
        compiler_params=pltpu.CompilerParams(vmem_limit_bytes=16 << 20),
        cost_estimate=pl.CostEstimate(flops=4 * 10**9, bytes_accessed=4 << 20, transcendentals=0),
        name="merge",
    )(where, mix, own, *others)


def start_weights(kernel_ref, weights, sems):
    chans = weights.shape[1]
    for t in range(9):
        pltpu.make_async_copy(
            kernel_ref.at[pl.ds(t * chans, chans)], weights.at[t], sems.at[t]
        ).start()


def tap_sums(patch, weights, sems, totals):
    for t in range(9):
        arrived(weights.at[t], sems.at[t])
        terms = [
            mm(patch(0, t // 3, t % 3), weights[t]),
            lax.dot_general(
                patch(1, 2 - t // 3, 2 - t % 3), weights[t], NT, preferred_element_type=F32
            ),
        ]
        for n, term in enumerate(terms):
            totals[n] = totals[n] + term if t else term


def conv_kernel(rows, kernel_ref, feat_ref, grad_ref, above_ref, below_ref, west_ref, east_ref, out_ref, back_ref, raw, lo, hi, sides, weights, totals, sems):
    pixels, chans = feat_ref.shape
    cols = pixels // rows
    loads = [
        (feat_ref, raw.at[0, pl.ds(cols, pixels)]),
        (grad_ref, raw.at[1, pl.ds(cols, pixels)]),
        (west_ref, sides.at[0]),
        (east_ref, sides.at[1]),
    ]
    for k, ref in enumerate((above_ref, below_ref)):
        for n in range(2):
            part = raw.at[n, pl.ds(k * (cols + pixels), cols)]
            loads.append((ref.at[pl.ds(n * cols, cols)], part))
        loads.append((ref.at[pl.ds(2 * cols, 2 * rows)], sides.at[2 + k]))
    loads = [pltpu.make_async_copy(*load, sems.at[9 + n]) for n, load in enumerate(loads)]
    for copy in loads:
        copy.start()
    start_weights(kernel_ref, weights, sems)
    for copy in loads:
        copy.wait()
    west, east, above, below = [sides[n].astype(F32) for n in range(4)]
    for n in range(2):
        mine = slice(n * rows, (n + 1) * rows)
        corner = [2 * n, 2 * n + 1]
        side = jnp.concatenate(
            [
                piece
                for k, cells in zip(corner, (west, east))
                for piece in (above[k : k + 1], cells[mine], below[k : k + 1])
            ],
            axis=0,
        )
        for h in range(rows + 2):
            shift_row(raw.at[n], lo.at[n], hi.at[n], h, cols, side)

    def patch(n, a, b):
        return (lo, raw, hi)[b][n, a * cols : a * cols + pixels]

    tap_sums(patch, weights, sems, totals)
    for n, ref in enumerate((out_ref, back_ref)):
        ref[...] = totals[n].astype(BF16)


def convolutions(kernel, feat, grad, beyond, near, rows):
    pixels, chans = feat.shape
    cols = pixels // rows
    block = jax.ShapeDtypeStruct((pixels, chans), BF16)
    maps = pltpu.VMEM((2, pixels + 2 * cols, chans), BF16)
    return pl.pallas_call(
        functools.partial(conv_kernel, rows),
        out_shape=[block, block],
        in_specs=[ANY] * 7,
        out_specs=[VMEM, VMEM],
        scratch_shapes=[
            maps,
            maps,
            maps,
            pltpu.VMEM((4, 2 * rows, chans), BF16),
            pltpu.VMEM((9, chans, chans), BF16),
            pltpu.VMEM((2, pixels, chans), F32),
            pltpu.SemaphoreType.DMA((19,)),
        ],
        compiler_params=pltpu.CompilerParams(vmem_limit_bytes=16 << 20),
        cost_estimate=pl.CostEstimate(flops=6 * 10**9, bytes_accessed=6 << 20, transcendentals=0),
        name="convolutions",
    )(*placed([kernel, feat, grad] + beyond + near))


def tap_term(maps, slot_row, t, grad):
    pixels, cols = grad.shape[0], maps[3]
    start = pl.multiple_of((slot_row + 1) * pixels + (t // 3 - 1) * cols, cols)
    return lax.dot_general(
        maps[t % 3][pl.ds(start, pixels), :],
        grad[...],
        (((0,), (0,)), ((), ())),
        preferred_element_type=F32,
    )


def early_filter_kernel(rows, share, slots_ref, *refs):
    *maps, lo, raw, hi, total, ends, grad, sems = refs
    known = grad.shape[0]
    feats, grads = maps[:-known], maps[-known:]
    count = len(feats) - 1
    pixels, lanes = raw.shape[1:]
    cols = pixels // rows
    window = pl.multiple_of(slots_ref[0] * share // lanes * lanes, lanes)
    cut = pl.ds(window, lanes)
    for i in range(count):
        j = slots_ref[i] + 1
        start_map(feats, i, raw.at[j], sems.at[0], cut)
        start_rest(feats, i, ends.at[j], sems.at[1], cut)
    for i, ref in enumerate(grads):
        pltpu.make_async_copy(ref, grad.at[i], sems.at[2]).start()
    inside = pl.ds(1, count)
    arrived(raw.at[inside], sems.at[0])
    arrived(ends.at[inside], sems.at[1])
    for j, h in ((0, rows - 1), (count + 1, 0)):
        for ref in (raw, lo, hi):
            ref[j, h * cols : (h + 1) * cols] = jnp.zeros((cols, lanes), BF16)
    for j in range(1, count + 1):
        side = ends[j].astype(F32)
        for h in range(rows):
            shift_row(raw.at[j], lo.at[j], hi.at[j], h, cols, side)
    arrived(grad, sems.at[2])
    flat = [ref.reshape((count + 2) * pixels, lanes) for ref in (lo, raw, hi)] + [cols]
    for t in range(9):
        terms = [tap_term(flat, slots_ref[i], t, grad.at[i]) for i in range(known)]
        total[t] = functools.reduce(jnp.add, terms)


def early_filter(slots, feats, grads, rows, share):
    pixels, chans = grads[0].shape
    count, lanes = len(feats) - 1, 128
    window = jax.ShapeDtypeStruct((count + 2, pixels, lanes), BF16)
    inputs = feats + grads
    return pl.pallas_call(
        functools.partial(early_filter_kernel, rows, share),
        out_shape=[window] * 3 + [jax.ShapeDtypeStruct((9, lanes, chans), F32)],
        in_specs=[SMEM] + [ANY] * len(inputs),
        out_specs=[VMEM] * 4,
        scratch_shapes=[
            pltpu.VMEM((count + 2, 2 * rows, lanes), BF16),
            pltpu.VMEM((len(grads), pixels, chans), BF16),
            pltpu.SemaphoreType.DMA((3,)),
        ],
        compiler_params=pltpu.CompilerParams(vmem_limit_bytes=(12 + count) << 20),
        cost_estimate=pl.CostEstimate(flops=4 * 10**9, bytes_accessed=4 << 20, transcendentals=0),
        name="early_filter",
    )(slots, *placed(inputs))


def late_filter_kernel(known, rows, where_ref, slots_ref, lo, raw, hi, early_ref, *refs):
    *grads, keep_ref, give_ref, grad, total, sem = refs
    pixels, lanes = raw.shape[1:]
    cols = pixels // rows
    pieces, taps, share, width = keep_ref.shape
    inner = pl.multiple_of(slots_ref[0] * share % lanes, 8)
    core = where_ref[1]
    for i in range(grad.shape[0]):
        start_map(grads, i, grad.at[i], sem)
    arrived(grad, sem)
    flat = [ref.reshape(raw.shape[0] * pixels, lanes) for ref in (lo, raw, hi)] + [cols]
    for t in range(9):
        terms = [
            tap_term(flat, slots_ref[known + i], t, grad.at[i]) for i in range(grad.shape[0])
        ]
        total[...] = functools.reduce(jnp.add, terms, early_ref[t])
        mine = total[pl.ds(inner, share), :]
        for i in range(pieces):
            even = mine[:, 2 * i * width : (2 * i + 1) * width]
            odd = mine[:, (2 * i + 1) * width : (2 * i + 2) * width]
            keep_ref[i, t] = jnp.where(core == 0, even, odd)
            give_ref[i, t] = jnp.where(core == 0, odd, even).astype(BF16)


def late_filter(where, slots, early, grads, known, rows, share, col_count):
    count = len(grads) - 1
    pixels, lanes = early[0].shape[1:]
    chans = early[3].shape[2]
    shape = (col_count // 2, 9, share, chans // col_count)
    return pl.pallas_call(
        functools.partial(late_filter_kernel, known, rows),
        out_shape=[jax.ShapeDtypeStruct(shape, F32), jax.ShapeDtypeStruct(shape, BF16)],
        in_specs=[SMEM, SMEM] + [VMEM] * 4 + [ANY] * len(grads),
        out_specs=[VMEM] * 2,
        scratch_shapes=[
            pltpu.VMEM((count, pixels, chans), BF16),
            pltpu.VMEM((lanes, chans), F32),
            pltpu.SemaphoreType.DMA,
        ],
        compiler_params=pltpu.CompilerParams(vmem_limit_bytes=(16 + count) << 20),
        cost_estimate=pl.CostEstimate(flops=2 * 10**9, bytes_accessed=4 << 20, transcendentals=0),
        name="late_filter",
    )(where, slots, *early, *placed(grads))


def edge_kernel(rows, feat_ref, grad_ref, first_ref, last_ref, maps, sems):
    cols = maps.shape[1] // rows
    loads = [
        pltpu.make_async_copy(ref, maps.at[n], sems.at[n])
        for n, ref in enumerate((feat_ref, grad_ref))
    ]
    for copy in loads:
        copy.start()
    for copy in loads:
        copy.wait()
    for out, at in ((first_ref, 0), (last_ref, cols - 1)):
        cells = [
            maps[n, h * cols + at : h * cols + at + 1, :].astype(F32)
            for n in range(2)
            for h in range(rows)
        ]
        out[...] = jnp.concatenate(cells, axis=0).astype(BF16)


def edges(feat, grad, rows):
    edge = jax.ShapeDtypeStruct((2 * rows, feat.shape[1]), BF16)
    return pl.pallas_call(
        functools.partial(edge_kernel, rows),
        out_shape=[edge, edge],
        in_specs=[ANY, ANY],
        out_specs=[VMEM, VMEM],
        scratch_shapes=[pltpu.VMEM((2,) + feat.shape, BF16), pltpu.SemaphoreType.DMA((2,))],
        name="edges",
    )(*placed([feat, grad]))


def ring_row(place, count):
    return jnp.where(place < count // 2, 2 * place, 2 * (count - 1 - place) + 1)


def ring_place(row, count):
    return jnp.where(row % 2 == 0, row // 2, count - 1 - row // 2)


def after(value, *earlier):
    return lax.optimization_barrier((value,) + earlier)[0]


def body(features, kernel, out_grad, projector, mixers):
    rows, cols, chans = features.shape
    row_count, col_count = lax.axis_size("rows"), lax.axis_size("cols")
    row, col = lax.axis_index("rows"), lax.axis_index("cols")
    rank = projector.shape[0]
    levels = col_count.bit_length() - 1
    half_way, pixels = row_count // 2, rows * cols

    order = list(range(0, row_count, 2)) + list(range(row_count - 1, 0, -2))
    east = [(i, i + 1) for i in range(col_count - 1)]
    west = [(j, i) for i, j in east]
    steps = [0] + [d for s in range(1, half_way) for d in (-s, s)] + [half_way]
    place = ring_place(row, row_count)
    slots = jnp.stack([ring_row((place + d) % row_count, row_count) for d in steps]).astype(jnp.int32)
    where = jnp.stack([row, col % 2, col, row]).astype(jnp.int32)

    def send(value, d):
        hop = [(order[i], order[(i + d) % row_count]) for i in range(row_count)]
        return lax.ppermute(value, "rows", hop)

    flat, own_grad = features.reshape(pixels, chans), out_grad.reshape(pixels, chans)
    first, last = edges(flat, own_grad, rows)
    near = [lax.ppermute(last, "cols", east), lax.ppermute(first, "cols", west)]
    packed = rank * pixels // chans
    tail = [projector[n : n + packed] for n in range(0, rank, packed)]
    message = jnp.concatenate([flat, jnp.concatenate(tail, axis=1)], axis=0)
    message = jnp.pad(message, ((0, 2 * rows), (0, 0)))
    message = lax.optimization_barrier(message)
    size = message.shape[0]
    sides = jnp.concatenate([x[:rows] for x in near])
    message = lax.dynamic_update_slice(message, sides, (size - 2 * rows, 0))
    feats = {0: message}
    beyond = []
    south = [(i, i + 1) for i in range(row_count - 1)]
    north = [(j, i) for i, j in south]
    for h, perm in ((rows - 1, south), (0, north)):
        cells = [x[n * rows + h : n * rows + h + 1] for n in range(2) for x in near]
        row_of = [x[h * cols : (h + 1) * cols] for x in (flat, own_grad)]
        parcel = jnp.concatenate(row_of + cells)
        parcel = jnp.pad(parcel, ((0, 2 * rows - len(cells)), (0, 0)))
        beyond.append(lax.ppermute(parcel, "rows", perm))
    for s in range(1, half_way):
        for d in (1, -1):
            feats[-s * d] = send(feats[(1 - s) * d], d)
    output, grad_features = convolutions(kernel, flat, own_grad, beyond, near, rows)
    feats[1 - half_way], feats[half_way - 1], output, grad_features = lax.optimization_barrier(
        (feats[1 - half_way], feats[half_way - 1], output, grad_features)
    )
    top, bottom = feats[1 - half_way], feats[half_way - 1]
    mid = size // 32 * 16
    feats[half_way] = [send(top[:mid], 1), send(bottom[mid:], -1)]
    grads = {0: own_grad}
    late_grad = after(own_grad, top, bottom)
    for d in (1, 2):
        grads[-d], grads[d] = send(late_grad, d), send(late_grad, -d)

    def listed(found, split=False):
        values = [found[d] for d in steps]
        return values[:-1] + list(values[-1]) if split else values

    feats = listed(feats, True)
    groups = [
        row_tree(slots, mixers[0], feats, start, rows, pixels)
        for start in range(0, row_count, GROUP)
    ]
    while len(groups) > 1:
        straight = where.at[0].set(0)
        groups = [
            merge(straight, mixers[0], groups[i], [groups[i + 1]])[0]
            for i in range(0, len(groups), 2)
        ]
    sketch = groups[0]

    def swap(value, level):
        return lax.ppermute(value, "cols", [(i, i ^ 1 << level) for i in range(col_count)])

    def turn(level):
        return where.at[0].set(col >> level & 1)

    swapped = swap(after(sketch, grads[1], grads[-1], grads[2], grads[-2]), 0)
    grads[-2], grads[2], _ = lax.optimization_barrier((grads[-2], grads[2], sketch))
    for s in range(3, half_way):
        for d in (1, -1):
            grads[-s * d] = send(grads[(1 - s) * d], d)
    result = merge(turn(0), mixers[1], sketch, [swapped])
    sketch, half = result
    top, bottom, _ = lax.optimization_barrier((grads[1 - half_way], grads[half_way - 1], half))
    split, known = pixels // 2, 5
    grads[half_way] = [send(top[:split], 1), send(bottom[split:], -1)]
    grads = listed(grads, True)
    share = chans // row_count
    early = early_filter(after(slots, half), feats, grads[:known], rows, share)
    terms, give = late_filter(where, slots, early, grads[known:], known, rows, share, col_count)
    filtered = give
    for level in range(levels):
        if level:
            pairs = terms.reshape((-1, 2) + terms.shape[1:])
            bit = col >> level & 1
            terms = lax.dynamic_index_in_dim(pairs, bit, 1, keepdims=False)
            give = lax.dynamic_index_in_dim(pairs, 1 - bit, 1, keepdims=False).astype(BF16)
        got = swap(give, level)
        if level < levels - 1:
            terms = terms + got.astype(F32)

    for level in range(1, levels):
        mine = swap(half, level)
        if level == 1:
            mine = after(mine, filtered)
        others = [mine, swap(mine, 0)]
        final = level == levels - 1
        share = (rank // col_count, sketch.shape[1] // row_count) if final else None
        result = merge(turn(level), mixers[1], sketch, others, share)
        sketch = result[0]
        if not final:
            half = result[1]
    grad_kernel = (terms + after(got, sketch).astype(F32))[0]
    return (
        output.reshape(features.shape),
        grad_features.reshape(features.shape),
        grad_kernel,
        sketch,
    )


def solution(mesh):
    in_specs = (P("rows", "cols", None), P(), P("rows", "cols", None), P("rows", "cols"), P())
    out_specs = (
        P("rows", "cols", None),
        P("rows", "cols", None),
        P(None, "rows", "cols"),
        P("cols", "rows"),
    )
    return jax.shard_map(body, mesh=mesh, in_specs=in_specs, out_specs=out_specs, check_vma=False)
```

```python
import functools
import jax
import jax.numpy as jnp
from jax import lax
from jax.experimental import pallas as pl
from jax.experimental.pallas import tpu as pltpu
from jax.sharding import PartitionSpec as P

NS_STEPS = 5
GROUP = 8
NT = (((1,), (1,)), ((), ()))
F32, BF16 = jnp.float32, jnp.bfloat16
VMEM = pl.BlockSpec(memory_space=pltpu.VMEM)
SMEM = pl.BlockSpec(memory_space=pltpu.SMEM)
ANY = pl.BlockSpec(memory_space=pltpu.HBM)


def mm(a, b):
    return jnp.dot(a, b, preferred_element_type=F32)


def spectral(grams):
    size = grams[0].shape[0]
    rows = lax.broadcasted_iota(jnp.int32, (size, size), 0)
    cols = lax.broadcasted_iota(jnp.int32, (size, size), 1)
    diagonal = rows == cols

    def total(x):
        return jnp.sum(jnp.sum(x, axis=1, keepdims=True), axis=0, keepdims=True)

    spreads = []
    for gram in grams:
        trace = total(jnp.where(diagonal, gram, 0.0))
        spread = gram / (trace + 1e-06) - jnp.where(diagonal, 1.0 / size, 0.0)
        spreads.append(spread / (jnp.sqrt(total(spread * spread)) + 1e-06))
    for sweep in range(NS_STEPS - 1):
        low = [y.astype(BF16) for y in spreads]
        squares = [mm(y, y).astype(BF16) for y in low]
        spreads = [1.5 * s - 0.5 * mm(y, z) for s, y, z in zip(spreads, low, squares)]
    return spreads


def combiner(mix, spread):
    low = spread.astype(BF16)
    square = mm(low, low).astype(BF16)
    once = mm(mix, low)
    turned = 1.5 * once - 0.5 * mm(once.astype(BF16), square)
    return (0.5 * (mix.astype(F32) + turned)).astype(BF16)


def gram_terms(parts):
    total = None
    for part in parts:
        term = lax.dot_general(part, part, NT, preferred_element_type=F32)
        total = term if total is None else total + term
    return total


def shifted(block, left, right):
    at = lax.broadcasted_iota(jnp.int32, block.shape, 0)
    wide = block.astype(F32)
    size = block.shape[0]
    low = jnp.where(at == 0, left, pltpu.roll(wide, 1, 0)).astype(BF16)
    high = jnp.where(at == size - 1, right, pltpu.roll(wide, size - 1, 0)).astype(BF16)
    return low, high


def rows_at(src, j, a, cols):
    size = src.shape[1]
    if a == 1:
        return src[j]
    if a == 0:
        return jnp.concatenate([src[j - 1, size - cols : size], src[j, : size - cols]], axis=0)
    return jnp.concatenate([src[j, cols:size], src[j + 1, :cols]], axis=0)


def shift_row(raw, lo, hi, h, cols, side):
    rows = side.shape[0] // 2
    at = slice(h * cols, (h + 1) * cols)
    lo[at], hi[at] = shifted(raw[at], side[h : h + 1], side[rows + h : rows + h + 1])


def placed(values):
    return [pltpu.with_memory_space_constraint(x, pltpu.HBM) for x in values]


def start_map(refs, i, target, sem, cut=slice(None)):
    size = target.shape[0]
    if i < len(refs) - 2:
        pltpu.make_async_copy(refs[i].at[pl.ds(0, size), cut], target, sem).start()
    else:
        mid = refs[-2].shape[0]
        pltpu.make_async_copy(refs[-2].at[:, cut], target.at[pl.ds(0, mid)], sem).start()
        pltpu.make_async_copy(refs[-1].at[pl.ds(0, size - mid), cut], target.at[pl.ds(mid, size - mid)], sem).start()


def start_rest(refs, i, ends, sem, cut=slice(None), proj=None, proj_sem=None):
    ref = refs[i] if i < len(refs) - 2 else refs[-1]
    size = ends.shape[0]
    below = ref.shape[0] - size
    if proj is None:
        pltpu.make_async_copy(ref.at[pl.ds(below, size), cut], ends, sem).start()
        return
    rank, pixels = proj.shape
    packed = rank * pixels // ref.shape[1]
    below -= packed
    for n in range(rank // packed):
        part = ref.at[pl.ds(below, packed), pl.ds(n * pixels, pixels)]
        pltpu.make_async_copy(part, proj.at[pl.ds(n * packed, packed)], proj_sem).start()


def arrived(target, sem):
    pltpu.make_async_copy(target, target, sem).wait()


def row_tree_kernel(first, step, rows, rows_ref, mix_ref, *refs):
    feats = refs[:-8]
    count = len(feats) - 1
    out_ref, raw, lo, hi, ends, proj, sk, sems = refs[-8:]
    blocks, pixels, chans = raw.shape
    cols = pixels // rows
    rank = proj.shape[1]

    for i in range(count):
        j = rows_ref[i] - first + 1

        @pl.when((j >= 0) & (j < blocks))
        def fetch(i=i, j=j):
            start_map(feats, i, raw.at[j], sems.at[0, j])
            start_rest(feats, i, ends.at[j], sems.at[1, j])

        @pl.when((j >= 1) & (j < blocks - 1))
        def fetch_projector(i=i, j=j):
            start_rest(feats, i, ends.at[j], None, slice(None), proj.at[j], sems.at[2, j])

    def ready(j, wanted):
        if 0 <= first + j - 1 < count:
            arrived(raw.at[j], sems.at[0, j])
            arrived(ends.at[j], sems.at[1, j])
            side = ends[j].astype(F32)
            for h in wanted:
                shift_row(raw.at[j], lo.at[j], hi.at[j], h, cols, side)
        else:
            for h in wanted:
                for ref in (raw, lo, hi):
                    ref[j, h * cols : (h + 1) * cols] = jnp.zeros((cols, chans), BF16)

    ready(0, (rows - 1,))
    ready(1, range(rows))
    for j in range(1, blocks - 1):
        ready(j + 1, range(rows) if j + 1 < blocks - 1 else (0,))
        arrived(proj.at[j], sems.at[2, j])
        half, part = divmod(j - 1, 2)
        for a in range(3):
            for b, src in enumerate((lo, raw, hi)):
                t = 3 * a + b
                sk[half, part * rank : (part + 1) * rank, t * chans : (t + 1) * chans] = mm(
                    proj[j], rows_at(src, j, a, cols)
                ).astype(BF16)
    mix = mix_ref[...]
    left = (blocks - 2) // 2
    width = sk.shape[-1]
    starts = range(0, width, step)
    while left:
        spreads = spectral(
            [gram_terms(sk[i, :, s : s + step] for s in starts) for i in range(left)]
        )
        for i in range(left):
            mixed = combiner(mix, spreads[i])
            for s in starts:
                piece = mm(mixed, sk[i, :, s : s + step]).astype(BF16)
                if left == 1:
                    out_ref[:, s : s + step] = piece
                else:
                    sk[i // 2, (i % 2) * rank : (i % 2 + 1) * rank, s : s + step] = piece
        left //= 2


def row_tree(slots, mix, feats, first, rows, pixels):
    chans = feats[0].shape[1]
    rank = mix.shape[0]
    width = 9 * chans
    blocks = GROUP + 2
    maps = pltpu.VMEM((blocks, pixels, chans), BF16)
    return pl.pallas_call(
        functools.partial(row_tree_kernel, first, 1536, rows),
        out_shape=jax.ShapeDtypeStruct((rank, width), BF16),
        in_specs=[SMEM, VMEM] + [ANY] * len(feats),
        out_specs=VMEM,
        scratch_shapes=[
            maps,
            maps,
            maps,
            pltpu.VMEM((blocks, 2 * rows, chans), BF16),
            pltpu.VMEM((blocks, rank, pixels), BF16),
            pltpu.VMEM((GROUP // 2, 2 * rank, width), BF16),
            pltpu.SemaphoreType.DMA((3, blocks)),
        ],
        compiler_params=pltpu.CompilerParams(vmem_limit_bytes=48 << 20),
        cost_estimate=pl.CostEstimate(flops=2 * 10**10, bytes_accessed=8 << 20, transcendentals=0),
        name="row_tree",
    )(slots, mix, *placed(feats))


def own_columns(where_ref, own, others, mixed, out_ref):
    share = out_ref.shape[1]
    half = own.shape[1] // 2
    window = (share + 2 * 127) // 128 * 128
    start = where_ref[3] * share
    which = start // half
    inner = start - which * half
    base = pl.multiple_of(jnp.minimum(inner // 128 * 128, half - window), 128)
    core = where_ref[1]
    near = others[0][:, pl.ds(base, window)].astype(F32)
    far = others[1][:, pl.ds(base, window)].astype(F32)
    other = jnp.where(core == which, near, far).astype(BF16)
    part = jnp.concatenate([own[:, pl.ds(pl.multiple_of(which * half + base, 128), window)], other], axis=0)
    value = mm(mixed, part)
    value = pltpu.roll(value, (window - (inner - base)) % window, 1)
    out_ref[...] = value[:, :share].astype(BF16)


def merge_kernel(step, halves, share, where_ref, mix_ref, *refs):
    rank, width = refs[0].shape
    own = refs[0]
    others = refs[1 : 2 + halves]
    outs = refs[2 + halves :]
    if not share:
        *outs, merged, sem = outs
    half = width // 2
    core = where_ref[1]

    def spans():
        for s in range(0, width, step):
            if halves:
                which, inner = divmod(s, half)
                place = pl.multiple_of((core + which) % 2 * half + inner, 128)
                other = others[which][:, inner : inner + step]
            else:
                place, other = s, others[0][:, s : s + step]
            yield place, jnp.concatenate([own[:, pl.ds(place, step)], other], axis=0)

    spread = spectral([gram_terms(part for _, part in spans())])[0]
    if share:
        mix = mix_ref[pl.ds(pl.multiple_of(where_ref[2] * share, 16), share), :]
    else:
        mix = mix_ref[...]
    turned = jnp.concatenate([mix[:, rank:], mix[:, :rank]], axis=1)
    mix = jnp.where(where_ref[0] == 0, mix.astype(F32), turned.astype(F32)).astype(BF16)
    mixed = combiner(mix, spread)
    if share:
        own_columns(where_ref, own, others, mixed, outs[0])
        return
    for place, part in spans():
        span = pl.ds(place, step)
        merged[:, span] = mm(mixed, part).astype(BF16)
        pltpu.make_async_copy(merged.at[:, span], outs[0].at[:, span], sem).start()
    outs[1][...] = merged[:, pl.ds(pl.multiple_of(core * half, 128), half)]
    pltpu.make_async_copy(merged, outs[0], sem).wait()


def merge(where, mix, own, others, share=None):
    rank, width = own.shape
    if share:
        shapes = [jax.ShapeDtypeStruct(share, BF16)]
    else:
        shapes = [pltpu.HBM((rank, width), BF16), jax.ShapeDtypeStruct((rank, width // 2), BF16)]
    return pl.pallas_call(
        functools.partial(merge_kernel, 1152, len(others) == 2, share[0] if share else 0),
        out_shape=shapes,
        in_specs=[SMEM] + [VMEM] * (2 + len(others)),
        out_specs=[VMEM] if share else [ANY, VMEM],
        scratch_shapes=() if share else (pltpu.VMEM((rank, width), BF16), pltpu.SemaphoreType.DMA),
        compiler_params=pltpu.CompilerParams(vmem_limit_bytes=16 << 20),
        cost_estimate=pl.CostEstimate(flops=4 * 10**9, bytes_accessed=4 << 20, transcendentals=0),
        name="merge",
    )(where, mix, own, *others)


def start_weights(kernel_ref, weights, sems):
    chans = weights.shape[1]
    for t in range(9):
        pltpu.make_async_copy(
            kernel_ref.at[pl.ds(t * chans, chans)], weights.at[t], sems.at[t]
        ).start()


def tap_sums(patch, weights, sems, totals):
    for t in range(9):
        arrived(weights.at[t], sems.at[t])
        terms = [
            mm(patch(0, t // 3, t % 3), weights[t]),
            lax.dot_general(
                patch(1, 2 - t // 3, 2 - t % 3), weights[t], NT, preferred_element_type=F32
            ),
        ]
        for n, term in enumerate(terms):
            totals[n] = totals[n] + term if t else term


def conv_kernel(rows, kernel_ref, feat_ref, grad_ref, above_ref, below_ref, west_ref, east_ref, out_ref, back_ref, raw, lo, hi, sides, weights, totals, sems):
    pixels, chans = feat_ref.shape
    cols = pixels // rows
    loads = [
        (feat_ref, raw.at[0, pl.ds(cols, pixels)]),
        (grad_ref, raw.at[1, pl.ds(cols, pixels)]),
        (west_ref, sides.at[0]),
        (east_ref, sides.at[1]),
    ]
    for k, ref in enumerate((above_ref, below_ref)):
        for n in range(2):
            part = raw.at[n, pl.ds(k * (cols + pixels), cols)]
            loads.append((ref.at[pl.ds(n * cols, cols)], part))
        loads.append((ref.at[pl.ds(2 * cols, 2 * rows)], sides.at[2 + k]))
    loads = [pltpu.make_async_copy(*load, sems.at[9 + n]) for n, load in enumerate(loads)]
    for copy in loads:
        copy.start()
    start_weights(kernel_ref, weights, sems)
    for copy in loads:
        copy.wait()
    west, east, above, below = [sides[n].astype(F32) for n in range(4)]
    for n in range(2):
        mine = slice(n * rows, (n + 1) * rows)
        corner = [2 * n, 2 * n + 1]
        side = jnp.concatenate(
            [
                piece
                for k, cells in zip(corner, (west, east))
                for piece in (above[k : k + 1], cells[mine], below[k : k + 1])
            ],
            axis=0,
        )
        for h in range(rows + 2):
            shift_row(raw.at[n], lo.at[n], hi.at[n], h, cols, side)

    def patch(n, a, b):
        return (lo, raw, hi)[b][n, a * cols : a * cols + pixels]

    tap_sums(patch, weights, sems, totals)
    for n, ref in enumerate((out_ref, back_ref)):
        ref[...] = totals[n].astype(BF16)


def convolutions(kernel, feat, grad, beyond, near, rows):
    pixels, chans = feat.shape
    cols = pixels // rows
    block = jax.ShapeDtypeStruct((pixels, chans), BF16)
    maps = pltpu.VMEM((2, pixels + 2 * cols, chans), BF16)
    return pl.pallas_call(
        functools.partial(conv_kernel, rows),
        out_shape=[block, block],
        in_specs=[ANY] * 7,
        out_specs=[VMEM, VMEM],
        scratch_shapes=[
            maps,
            maps,
            maps,
            pltpu.VMEM((4, 2 * rows, chans), BF16),
            pltpu.VMEM((9, chans, chans), BF16),
            pltpu.VMEM((2, pixels, chans), F32),
            pltpu.SemaphoreType.DMA((19,)),
        ],
        compiler_params=pltpu.CompilerParams(vmem_limit_bytes=16 << 20),
        cost_estimate=pl.CostEstimate(flops=6 * 10**9, bytes_accessed=6 << 20, transcendentals=0),
        name="convolutions",
    )(*placed([kernel, feat, grad] + beyond + near))


def tap_term(maps, slot_row, t, grad):
    pixels, cols = grad.shape[0], maps[3]
    start = pl.multiple_of((slot_row + 1) * pixels + (t // 3 - 1) * cols, cols)
    return lax.dot_general(
        maps[t % 3][pl.ds(start, pixels), :],
        grad[...],
        (((0,), (0,)), ((), ())),
        preferred_element_type=F32,
    )


def early_filter_kernel(rows, share, slots_ref, *refs):
    *maps, _, lo, raw, hi, total, ends, grad, sems = refs
    known = grad.shape[0]
    feats, grads = maps[:-known], maps[-known:]
    count = len(feats) - 1
    pixels, lanes = raw.shape[1:]
    cols = pixels // rows
    window = pl.multiple_of(slots_ref[0] * share // lanes * lanes, lanes)
    cut = pl.ds(window, lanes)
    for i in range(count):
        j = slots_ref[i] + 1
        start_map(feats, i, raw.at[j], sems.at[0], cut)
        start_rest(feats, i, ends.at[j], sems.at[1], cut)
    for i, ref in enumerate(grads):
        pltpu.make_async_copy(ref, grad.at[i], sems.at[2]).start()
    inside = pl.ds(1, count)
    arrived(raw.at[inside], sems.at[0])
    arrived(ends.at[inside], sems.at[1])
    for j, h in ((0, rows - 1), (count + 1, 0)):
        for ref in (raw, lo, hi):
            ref[j, h * cols : (h + 1) * cols] = jnp.zeros((cols, lanes), BF16)
    for j in range(1, count + 1):
        side = ends[j].astype(F32)
        for h in range(rows):
            shift_row(raw.at[j], lo.at[j], hi.at[j], h, cols, side)
    arrived(grad, sems.at[2])
    flat = [ref.reshape((count + 2) * pixels, lanes) for ref in (lo, raw, hi)] + [cols]
    for t in range(9):
        terms = [tap_term(flat, slots_ref[i], t, grad.at[i]) for i in range(known)]
        total[t] = functools.reduce(jnp.add, terms)


def early_filter(slots, feats, grads, met, rows, share):
    pixels, chans = grads[0].shape
    count, lanes = len(feats) - 1, 128
    window = jax.ShapeDtypeStruct((count + 2, pixels, lanes), BF16)
    inputs = feats + grads + [met]
    return pl.pallas_call(
        functools.partial(early_filter_kernel, rows, share),
        out_shape=[window] * 3 + [jax.ShapeDtypeStruct((9, lanes, chans), F32)],
        in_specs=[SMEM] + [ANY] * len(inputs),
        out_specs=[VMEM] * 4,
        scratch_shapes=[
            pltpu.VMEM((count + 2, 2 * rows, lanes), BF16),
            pltpu.VMEM((len(grads), pixels, chans), BF16),
            pltpu.SemaphoreType.DMA((3,)),
        ],
        compiler_params=pltpu.CompilerParams(vmem_limit_bytes=(12 + count) << 20),
        cost_estimate=pl.CostEstimate(flops=4 * 10**9, bytes_accessed=4 << 20, transcendentals=0),
        name="early_filter",
    )(slots, *placed(inputs))


def late_filter_kernel(known, rows, where_ref, slots_ref, lo, raw, hi, early_ref, *refs):
    *grads, keep_ref, give_ref, grad, total, sem = refs
    pixels, lanes = raw.shape[1:]
    cols = pixels // rows
    pieces, taps, share, width = keep_ref.shape
    inner = pl.multiple_of(slots_ref[0] * share % lanes, 8)
    core = where_ref[1]
    for i in range(grad.shape[0]):
        start_map(grads, i, grad.at[i], sem)
    arrived(grad, sem)
    flat = [ref.reshape(raw.shape[0] * pixels, lanes) for ref in (lo, raw, hi)] + [cols]
    for t in range(9):
        terms = [
            tap_term(flat, slots_ref[known + i], t, grad.at[i]) for i in range(grad.shape[0])
        ]
        total[...] = functools.reduce(jnp.add, terms, early_ref[t])
        mine = total[pl.ds(inner, share), :]
        for i in range(pieces):
            even = mine[:, 2 * i * width : (2 * i + 1) * width]
            odd = mine[:, (2 * i + 1) * width : (2 * i + 2) * width]
            keep_ref[i, t] = jnp.where(core == 0, even, odd)
            give_ref[i, t] = jnp.where(core == 0, odd, even).astype(BF16)


def late_filter(where, slots, early, grads, known, rows, share, col_count):
    count = len(grads) - 1
    pixels, lanes = early[0].shape[1:]
    chans = early[3].shape[2]
    shape = (col_count // 2, 9, share, chans // col_count)
    return pl.pallas_call(
        functools.partial(late_filter_kernel, known, rows),
        out_shape=[jax.ShapeDtypeStruct(shape, F32), jax.ShapeDtypeStruct(shape, BF16)],
        in_specs=[SMEM, SMEM] + [VMEM] * 4 + [ANY] * len(grads),
        out_specs=[VMEM] * 2,
        scratch_shapes=[
            pltpu.VMEM((count, pixels, chans), BF16),
            pltpu.VMEM((lanes, chans), F32),
            pltpu.SemaphoreType.DMA,
        ],
        compiler_params=pltpu.CompilerParams(vmem_limit_bytes=(16 + count) << 20),
        cost_estimate=pl.CostEstimate(flops=2 * 10**9, bytes_accessed=4 << 20, transcendentals=0),
        name="late_filter",
    )(where, slots, *early, *placed(grads))


def edge_kernel(rows, feat_ref, grad_ref, first_ref, last_ref, maps, sems):
    cols = maps.shape[1] // rows
    loads = [
        pltpu.make_async_copy(ref, maps.at[n], sems.at[n])
        for n, ref in enumerate((feat_ref, grad_ref))
    ]
    for copy in loads:
        copy.start()
    for copy in loads:
        copy.wait()
    for out, at in ((first_ref, 0), (last_ref, cols - 1)):
        cells = [
            maps[n, h * cols + at : h * cols + at + 1, :].astype(F32)
            for n in range(2)
            for h in range(rows)
        ]
        out[...] = jnp.concatenate(cells, axis=0).astype(BF16)


def edges(feat, grad, rows):
    edge = jax.ShapeDtypeStruct((2 * rows, feat.shape[1]), BF16)
    return pl.pallas_call(
        functools.partial(edge_kernel, rows),
        out_shape=[edge, edge],
        in_specs=[ANY, ANY],
        out_specs=[VMEM, VMEM],
        scratch_shapes=[pltpu.VMEM((2,) + feat.shape, BF16), pltpu.SemaphoreType.DMA((2,))],
        name="edges",
    )(*placed([feat, grad]))


def ring_row(place, count):
    return jnp.where(place < count // 2, 2 * place, 2 * (count - 1 - place) + 1)


def ring_place(row, count):
    return jnp.where(row % 2 == 0, row // 2, count - 1 - row // 2)


def after(value, *earlier):
    return lax.optimization_barrier((value,) + earlier)[0]


def body(features, kernel, out_grad, projector, mixers):
    rows, cols, chans = features.shape
    row_count, col_count = lax.axis_size("rows"), lax.axis_size("cols")
    row, col = lax.axis_index("rows"), lax.axis_index("cols")
    rank = projector.shape[0]
    levels = col_count.bit_length() - 1
    half_way, pixels = row_count // 2, rows * cols

    order = list(range(0, row_count, 2)) + list(range(row_count - 1, 0, -2))
    east = [(i, i + 1) for i in range(col_count - 1)]
    west = [(j, i) for i, j in east]
    steps = [0] + [d for s in range(1, half_way) for d in (-s, s)] + [half_way]
    place = ring_place(row, row_count)
    slots = jnp.stack([ring_row((place + d) % row_count, row_count) for d in steps]).astype(jnp.int32)
    where = jnp.stack([row, col % 2, col, row]).astype(jnp.int32)

    def send(value, d):
        hop = [(order[i], order[(i + d) % row_count]) for i in range(row_count)]
        return lax.ppermute(value, "rows", hop)

    flat, own_grad = features.reshape(pixels, chans), out_grad.reshape(pixels, chans)
    first, last = edges(flat, own_grad, rows)
    near = [lax.ppermute(last, "cols", east), lax.ppermute(first, "cols", west)]
    packed = rank * pixels // chans
    tail = [projector[n : n + packed] for n in range(0, rank, packed)]
    message = jnp.concatenate([flat, jnp.concatenate(tail, axis=1)], axis=0)
    message = jnp.pad(message, ((0, 2 * rows), (0, 0)))
    message = lax.optimization_barrier(message)
    size = message.shape[0]
    sides = jnp.concatenate([x[:rows] for x in near])
    message = lax.dynamic_update_slice(message, sides, (size - 2 * rows, 0))
    feats = {0: message}
    beyond = []
    south = [(i, i + 1) for i in range(row_count - 1)]
    north = [(j, i) for i, j in south]
    for h, perm in ((rows - 1, south), (0, north)):
        cells = [x[n * rows + h : n * rows + h + 1] for n in range(2) for x in near]
        row_of = [x[h * cols : (h + 1) * cols] for x in (flat, own_grad)]
        parcel = jnp.concatenate(row_of + cells)
        parcel = jnp.pad(parcel, ((0, 2 * rows - len(cells)), (0, 0)))
        beyond.append(lax.ppermute(parcel, "rows", perm))
    for s in range(1, half_way):
        for d in (1, -1):
            feats[-s * d] = send(feats[(1 - s) * d], d)
    output, grad_features = convolutions(kernel, flat, own_grad, beyond, near, rows)
    feats[1 - half_way], feats[half_way - 1], output, grad_features = lax.optimization_barrier(
        (feats[1 - half_way], feats[half_way - 1], output, grad_features)
    )
    top, bottom = feats[1 - half_way], feats[half_way - 1]
    mid = size // 32 * 16
    feats[half_way] = [send(top[:mid], 1), send(bottom[mid:], -1)]
    grads = {0: own_grad}
    pairs = [(i, i ^ 1) for i in range(col_count)]
    met = lax.ppermute(top[:16, :128], "cols", pairs)
    late_grad, met, *_ = lax.optimization_barrier((own_grad, met, top, bottom))
    for d in (1, 2):
        grads[-d], grads[d] = send(late_grad, d), send(late_grad, -d)

    def listed(found, split=False):
        values = [found[d] for d in steps]
        return values[:-1] + list(values[-1]) if split else values

    feats = listed(feats, True)
    groups = [
        row_tree(slots, mixers[0], feats, start, rows, pixels)
        for start in range(0, row_count, GROUP)
    ]
    while len(groups) > 1:
        straight = where.at[0].set(0)
        groups = [
            merge(straight, mixers[0], groups[i], [groups[i + 1]])[0]
            for i in range(0, len(groups), 2)
        ]
    sketch = groups[0]

    def swap(value, level):
        return lax.ppermute(value, "cols", [(i, i ^ 1 << level) for i in range(col_count)])

    def turn(level):
        return where.at[0].set(col >> level & 1)

    swapped = swap(after(sketch, grads[1], grads[-1], grads[2], grads[-2]), 0)
    grads[-2], grads[2], _ = lax.optimization_barrier((grads[-2], grads[2], sketch))
    for s in range(3, half_way):
        for d in (1, -1):
            grads[-s * d] = send(grads[(1 - s) * d], d)
    result = merge(turn(0), mixers[1], sketch, [swapped])
    sketch, half = result
    top, bottom, _ = lax.optimization_barrier((grads[1 - half_way], grads[half_way - 1], half))
    split, known = pixels // 2, 5
    grads[half_way] = [send(top[:split], 1), send(bottom[split:], -1)]
    grads = listed(grads, True)
    share = chans // row_count
    early = early_filter(after(slots, half), feats, grads[:known], met, rows, share)
    terms, give = late_filter(where, slots, early, grads[known:], known, rows, share, col_count)
    filtered = give
    for level in range(levels):
        if level:
            pairs = terms.reshape((-1, 2) + terms.shape[1:])
            bit = col >> level & 1
            terms = lax.dynamic_index_in_dim(pairs, bit, 1, keepdims=False)
            give = lax.dynamic_index_in_dim(pairs, 1 - bit, 1, keepdims=False).astype(BF16)
        got = swap(give, level)
        if level < levels - 1:
            terms = terms + got.astype(F32)

    for level in range(1, levels):
        mine = swap(half, level)
        if level == 1:
            mine = after(mine, filtered)
        others = [mine, swap(mine, 0)]
        final = level == levels - 1
        share = (rank // col_count, sketch.shape[1] // row_count) if final else None
        result = merge(turn(level), mixers[1], sketch, others, share)
        sketch = result[0]
        if not final:
            half = result[1]
    grad_kernel = (terms + after(got, sketch).astype(F32))[0]
    return (
        output.reshape(features.shape),
        grad_features.reshape(features.shape),
        grad_kernel,
        sketch,
    )


def solution(mesh):
    in_specs = (P("rows", "cols", None), P(), P("rows", "cols", None), P("rows", "cols"), P())
    out_specs = (
        P("rows", "cols", None),
        P("rows", "cols", None),
        P(None, "rows", "cols"),
        P("cols", "rows"),
    )
    return jax.shard_map(body, mesh=mesh, in_specs=in_specs, out_specs=out_specs, check_vma=False)
```

```python
import functools
import jax
import jax.numpy as jnp
from jax import lax
from jax.experimental import pallas as pl
from jax.experimental.pallas import tpu as pltpu
from jax.sharding import PartitionSpec as P

NS_STEPS = 5
GROUP = 8
NT = (((1,), (1,)), ((), ()))
F32, BF16 = jnp.float32, jnp.bfloat16
VMEM = pl.BlockSpec(memory_space=pltpu.VMEM)
SMEM = pl.BlockSpec(memory_space=pltpu.SMEM)
ANY = pl.BlockSpec(memory_space=pltpu.HBM)


def mm(a, b):
    return jnp.dot(a, b, preferred_element_type=F32)


def spectral(grams):
    size = grams[0].shape[0]
    rows = lax.broadcasted_iota(jnp.int32, (size, size), 0)
    cols = lax.broadcasted_iota(jnp.int32, (size, size), 1)
    diagonal = rows == cols

    def total(x):
        return jnp.sum(jnp.sum(x, axis=1, keepdims=True), axis=0, keepdims=True)

    spreads = []
    for gram in grams:
        trace = total(jnp.where(diagonal, gram, 0.0))
        spread = gram / (trace + 1e-06) - jnp.where(diagonal, 1.0 / size, 0.0)
        spreads.append(spread / (jnp.sqrt(total(spread * spread)) + 1e-06))
    for sweep in range(NS_STEPS - 1):
        low = [y.astype(BF16) for y in spreads]
        squares = [mm(y, y).astype(BF16) for y in low]
        spreads = [1.5 * s - 0.5 * mm(y, z) for s, y, z in zip(spreads, low, squares)]
    return spreads


def combiner(mix, spread):
    low = spread.astype(BF16)
    square = mm(low, low).astype(BF16)
    once = mm(mix, low)
    turned = 1.5 * once - 0.5 * mm(once.astype(BF16), square)
    return (0.5 * (mix.astype(F32) + turned)).astype(BF16)


def gram_terms(parts):
    total = None
    for part in parts:
        term = lax.dot_general(part, part, NT, preferred_element_type=F32)
        total = term if total is None else total + term
    return total


def shifted(block, left, right):
    at = lax.broadcasted_iota(jnp.int32, block.shape, 0)
    wide = block.astype(F32)
    size = block.shape[0]
    low = jnp.where(at == 0, left, pltpu.roll(wide, 1, 0)).astype(BF16)
    high = jnp.where(at == size - 1, right, pltpu.roll(wide, size - 1, 0)).astype(BF16)
    return low, high


def rows_at(src, j, a, cols):
    size = src.shape[1]
    if a == 1:
        return src[j]
    if a == 0:
        return jnp.concatenate([src[j - 1, size - cols : size], src[j, : size - cols]], axis=0)
    return jnp.concatenate([src[j, cols:size], src[j + 1, :cols]], axis=0)


def shift_row(raw, lo, hi, h, cols, side):
    rows = side.shape[0] // 2
    at = slice(h * cols, (h + 1) * cols)
    lo[at], hi[at] = shifted(raw[at], side[h : h + 1], side[rows + h : rows + h + 1])


def placed(values):
    return [pltpu.with_memory_space_constraint(x, pltpu.HBM) for x in values]


def start_map(refs, i, target, sem, cut=slice(None)):
    size = target.shape[0]
    if i < len(refs) - 2:
        pltpu.make_async_copy(refs[i].at[pl.ds(0, size), cut], target, sem).start()
    else:
        mid = refs[-2].shape[0]
        pltpu.make_async_copy(refs[-2].at[:, cut], target.at[pl.ds(0, mid)], sem).start()
        pltpu.make_async_copy(refs[-1].at[pl.ds(0, size - mid), cut], target.at[pl.ds(mid, size - mid)], sem).start()


def start_rest(refs, i, ends, sem, cut=slice(None), proj=None, proj_sem=None):
    ref = refs[i] if i < len(refs) - 2 else refs[-1]
    size = ends.shape[0]
    below = ref.shape[0] - size
    if proj is None:
        pltpu.make_async_copy(ref.at[pl.ds(below, size), cut], ends, sem).start()
        return
    rank, pixels = proj.shape
    packed = rank * pixels // ref.shape[1]
    below -= packed
    for n in range(rank // packed):
        part = ref.at[pl.ds(below, packed), pl.ds(n * pixels, pixels)]
        pltpu.make_async_copy(part, proj.at[pl.ds(n * packed, packed)], proj_sem).start()


def arrived(target, sem):
    pltpu.make_async_copy(target, target, sem).wait()


def row_tree_kernel(first, step, rows, rows_ref, mix_ref, *refs):
    feats = refs[:-8]
    count = len(feats) - 1
    out_ref, raw, lo, hi, ends, proj, sk, sems = refs[-8:]
    blocks, pixels, chans = raw.shape
    cols = pixels // rows
    rank = proj.shape[1]

    for i in range(count):
        j = rows_ref[i] - first + 1

        @pl.when((j >= 0) & (j < blocks))
        def fetch(i=i, j=j):
            start_map(feats, i, raw.at[j], sems.at[0, j])
            start_rest(feats, i, ends.at[j], sems.at[1, j])

        @pl.when((j >= 1) & (j < blocks - 1))
        def fetch_projector(i=i, j=j):
            start_rest(feats, i, ends.at[j], None, slice(None), proj.at[j], sems.at[2, j])

    def ready(j, wanted):
        if 0 <= first + j - 1 < count:
            arrived(raw.at[j], sems.at[0, j])
            arrived(ends.at[j], sems.at[1, j])
            side = ends[j].astype(F32)
            for h in wanted:
                shift_row(raw.at[j], lo.at[j], hi.at[j], h, cols, side)
        else:
            for h in wanted:
                for ref in (raw, lo, hi):
                    ref[j, h * cols : (h + 1) * cols] = jnp.zeros((cols, chans), BF16)

    ready(0, (rows - 1,))
    ready(1, range(rows))
    for j in range(1, blocks - 1):
        ready(j + 1, range(rows) if j + 1 < blocks - 1 else (0,))
        arrived(proj.at[j], sems.at[2, j])
        half, part = divmod(j - 1, 2)
        for a in range(3):
            for b, src in enumerate((lo, raw, hi)):
                t = 3 * a + b
                sk[half, part * rank : (part + 1) * rank, t * chans : (t + 1) * chans] = mm(
                    proj[j], rows_at(src, j, a, cols)
                ).astype(BF16)
    mix = mix_ref[...]
    left = (blocks - 2) // 2
    width = sk.shape[-1]
    starts = range(0, width, step)
    while left:
        spreads = spectral(
            [gram_terms(sk[i, :, s : s + step] for s in starts) for i in range(left)]
        )
        for i in range(left):
            mixed = combiner(mix, spreads[i])
            for s in starts:
                piece = mm(mixed, sk[i, :, s : s + step]).astype(BF16)
                if left == 1:
                    out_ref[:, s : s + step] = piece
                else:
                    sk[i // 2, (i % 2) * rank : (i % 2 + 1) * rank, s : s + step] = piece
        left //= 2


def row_tree(slots, mix, feats, first, rows, pixels):
    chans = feats[0].shape[1]
    rank = mix.shape[0]
    width = 9 * chans
    blocks = GROUP + 2
    maps = pltpu.VMEM((blocks, pixels, chans), BF16)
    return pl.pallas_call(
        functools.partial(row_tree_kernel, first, 1536, rows),
        out_shape=jax.ShapeDtypeStruct((rank, width), BF16),
        in_specs=[SMEM, VMEM] + [ANY] * (len(feats) - 2) + [pl.BlockSpec(memory_space=pl.ANY)] * 2,
        out_specs=VMEM,
        scratch_shapes=[
            maps,
            maps,
            maps,
            pltpu.VMEM((blocks, 2 * rows, chans), BF16),
            pltpu.VMEM((blocks, rank, pixels), BF16),
            pltpu.VMEM((GROUP // 2, 2 * rank, width), BF16),
            pltpu.SemaphoreType.DMA((3, blocks)),
        ],
        compiler_params=pltpu.CompilerParams(vmem_limit_bytes=48 << 20),
        cost_estimate=pl.CostEstimate(flops=2 * 10**10, bytes_accessed=8 << 20, transcendentals=0),
        name="row_tree",
    )(slots, mix, *placed(feats[:-2]), *feats[-2:])


def own_columns(where_ref, own, others, mixed, out_ref):
    share = out_ref.shape[1]
    half = own.shape[1] // 2
    window = (share + 2 * 127) // 128 * 128
    start = where_ref[3] * share
    which = start // half
    inner = start - which * half
    base = pl.multiple_of(jnp.minimum(inner // 128 * 128, half - window), 128)
    core = where_ref[1]
    near = others[0][:, pl.ds(base, window)].astype(F32)
    far = others[1][:, pl.ds(base, window)].astype(F32)
    other = jnp.where(core == which, near, far).astype(BF16)
    part = jnp.concatenate([own[:, pl.ds(pl.multiple_of(which * half + base, 128), window)], other], axis=0)
    value = mm(mixed, part)
    value = pltpu.roll(value, (window - (inner - base)) % window, 1)
    out_ref[...] = value[:, :share].astype(BF16)


def merge_kernel(step, halves, share, where_ref, mix_ref, *refs):
    rank, width = refs[0].shape
    own = refs[0]
    others = refs[1 : 2 + halves]
    outs = refs[2 + halves :]
    if not share:
        *outs, merged, sem = outs
    half = width // 2
    core = where_ref[1]

    def spans():
        for s in range(0, width, step):
            if halves:
                which, inner = divmod(s, half)
                place = pl.multiple_of((core + which) % 2 * half + inner, 128)
                other = others[which][:, inner : inner + step]
            else:
                place, other = s, others[0][:, s : s + step]
            yield place, jnp.concatenate([own[:, pl.ds(place, step)], other], axis=0)

    spread = spectral([gram_terms(part for _, part in spans())])[0]
    if share:
        mix = mix_ref[pl.ds(pl.multiple_of(where_ref[2] * share, 16), share), :]
    else:
        mix = mix_ref[...]
    turned = jnp.concatenate([mix[:, rank:], mix[:, :rank]], axis=1)
    mix = jnp.where(where_ref[0] == 0, mix.astype(F32), turned.astype(F32)).astype(BF16)
    mixed = combiner(mix, spread)
    if share:
        own_columns(where_ref, own, others, mixed, outs[0])
        return
    for place, part in spans():
        span = pl.ds(place, step)
        merged[:, span] = mm(mixed, part).astype(BF16)
        pltpu.make_async_copy(merged.at[:, span], outs[0].at[:, span], sem).start()
    outs[1][...] = merged[:, pl.ds(pl.multiple_of(core * half, 128), half)]
    pltpu.make_async_copy(merged, outs[0], sem).wait()


def merge(where, mix, own, others, share=None):
    rank, width = own.shape
    if share:
        shapes = [jax.ShapeDtypeStruct(share, BF16)]
    else:
        shapes = [pltpu.HBM((rank, width), BF16), jax.ShapeDtypeStruct((rank, width // 2), BF16)]
    return pl.pallas_call(
        functools.partial(merge_kernel, 1152, len(others) == 2, share[0] if share else 0),
        out_shape=shapes,
        in_specs=[SMEM] + [VMEM] * (2 + len(others)),
        out_specs=[VMEM] if share else [ANY, VMEM],
        scratch_shapes=() if share else (pltpu.VMEM((rank, width), BF16), pltpu.SemaphoreType.DMA),
        compiler_params=pltpu.CompilerParams(vmem_limit_bytes=16 << 20),
        cost_estimate=pl.CostEstimate(flops=4 * 10**9, bytes_accessed=4 << 20, transcendentals=0),
        name="merge",
    )(where, mix, own, *others)


def start_weights(kernel_ref, weights, sems):
    chans = weights.shape[1]
    for t in range(9):
        pltpu.make_async_copy(
            kernel_ref.at[pl.ds(t * chans, chans)], weights.at[t], sems.at[t]
        ).start()


def tap_sums(patch, weights, sems, totals):
    for t in range(9):
        arrived(weights.at[t], sems.at[t])
        terms = [
            mm(patch(0, t // 3, t % 3), weights[t]),
            lax.dot_general(
                patch(1, 2 - t // 3, 2 - t % 3), weights[t], NT, preferred_element_type=F32
            ),
        ]
        for n, term in enumerate(terms):
            totals[n] = totals[n] + term if t else term


def conv_kernel(rows, kernel_ref, feat_ref, grad_ref, above_ref, below_ref, west_ref, east_ref, out_ref, back_ref, raw, lo, hi, sides, weights, totals, sems):
    pixels, chans = feat_ref.shape
    cols = pixels // rows
    loads = [
        (feat_ref, raw.at[0, pl.ds(cols, pixels)]),
        (grad_ref, raw.at[1, pl.ds(cols, pixels)]),
        (west_ref, sides.at[0]),
        (east_ref, sides.at[1]),
    ]
    for k, ref in enumerate((above_ref, below_ref)):
        for n in range(2):
            part = raw.at[n, pl.ds(k * (cols + pixels), cols)]
            loads.append((ref.at[pl.ds(n * cols, cols)], part))
        loads.append((ref.at[pl.ds(2 * cols, 2 * rows)], sides.at[2 + k]))
    loads = [pltpu.make_async_copy(*load, sems.at[9 + n]) for n, load in enumerate(loads)]
    for copy in loads:
        copy.start()
    start_weights(kernel_ref, weights, sems)
    for copy in loads:
        copy.wait()
    west, east, above, below = [sides[n].astype(F32) for n in range(4)]
    for n in range(2):
        mine = slice(n * rows, (n + 1) * rows)
        corner = [2 * n, 2 * n + 1]
        side = jnp.concatenate(
            [
                piece
                for k, cells in zip(corner, (west, east))
                for piece in (above[k : k + 1], cells[mine], below[k : k + 1])
            ],
            axis=0,
        )
        for h in range(rows + 2):
            shift_row(raw.at[n], lo.at[n], hi.at[n], h, cols, side)

    def patch(n, a, b):
        return (lo, raw, hi)[b][n, a * cols : a * cols + pixels]

    tap_sums(patch, weights, sems, totals)
    for n, ref in enumerate((out_ref, back_ref)):
        ref[...] = totals[n].astype(BF16)


def convolutions(kernel, feat, grad, beyond, near, rows):
    pixels, chans = feat.shape
    cols = pixels // rows
    block = jax.ShapeDtypeStruct((pixels, chans), BF16)
    maps = pltpu.VMEM((2, pixels + 2 * cols, chans), BF16)
    return pl.pallas_call(
        functools.partial(conv_kernel, rows),
        out_shape=[block, block],
        in_specs=[ANY] * 7,
        out_specs=[VMEM, VMEM],
        scratch_shapes=[
            maps,
            maps,
            maps,
            pltpu.VMEM((4, 2 * rows, chans), BF16),
            pltpu.VMEM((9, chans, chans), BF16),
            pltpu.VMEM((2, pixels, chans), F32),
            pltpu.SemaphoreType.DMA((19,)),
        ],
        compiler_params=pltpu.CompilerParams(vmem_limit_bytes=16 << 20),
        cost_estimate=pl.CostEstimate(flops=6 * 10**9, bytes_accessed=6 << 20, transcendentals=0),
        name="convolutions",
    )(*placed([kernel, feat, grad] + beyond + near))


def tap_term(maps, slot_row, t, grad):
    pixels, cols = grad.shape[0], maps[3]
    start = pl.multiple_of((slot_row + 1) * pixels + (t // 3 - 1) * cols, cols)
    return lax.dot_general(
        maps[t % 3][pl.ds(start, pixels), :],
        grad[...],
        (((0,), (0,)), ((), ())),
        preferred_element_type=F32,
    )


def early_filter_kernel(rows, share, slots_ref, *refs):
    *maps, _, lo, raw, hi, total, ends, grad, sems = refs
    known = grad.shape[0]
    feats, grads = maps[:-known], maps[-known:]
    count = len(feats) - 1
    pixels, lanes = raw.shape[1:]
    cols = pixels // rows
    window = pl.multiple_of(slots_ref[0] * share // lanes * lanes, lanes)
    cut = pl.ds(window, lanes)
    for i in range(count):
        j = slots_ref[i] + 1
        start_map(feats, i, raw.at[j], sems.at[0], cut)
        start_rest(feats, i, ends.at[j], sems.at[1], cut)
    for i, ref in enumerate(grads):
        pltpu.make_async_copy(ref, grad.at[i], sems.at[2]).start()
    inside = pl.ds(1, count)
    arrived(raw.at[inside], sems.at[0])
    arrived(ends.at[inside], sems.at[1])
    for j, h in ((0, rows - 1), (count + 1, 0)):
        for ref in (raw, lo, hi):
            ref[j, h * cols : (h + 1) * cols] = jnp.zeros((cols, lanes), BF16)
    for j in range(1, count + 1):
        side = ends[j].astype(F32)
        for h in range(rows):
            shift_row(raw.at[j], lo.at[j], hi.at[j], h, cols, side)
    arrived(grad, sems.at[2])
    flat = [ref.reshape((count + 2) * pixels, lanes) for ref in (lo, raw, hi)] + [cols]
    for t in range(9):
        terms = [tap_term(flat, slots_ref[i], t, grad.at[i]) for i in range(known)]
        total[t] = functools.reduce(jnp.add, terms)


def early_filter(slots, feats, grads, met, rows, share):
    pixels, chans = grads[0].shape
    count, lanes = len(feats) - 1, 128
    window = jax.ShapeDtypeStruct((count + 2, pixels, lanes), BF16)
    inputs = feats + grads + [met]
    return pl.pallas_call(
        functools.partial(early_filter_kernel, rows, share),
        out_shape=[window] * 3 + [jax.ShapeDtypeStruct((9, lanes, chans), F32)],
        in_specs=[SMEM] + [ANY] * len(inputs),
        out_specs=[VMEM] * 4,
        scratch_shapes=[
            pltpu.VMEM((count + 2, 2 * rows, lanes), BF16),
            pltpu.VMEM((len(grads), pixels, chans), BF16),
            pltpu.SemaphoreType.DMA((3,)),
        ],
        compiler_params=pltpu.CompilerParams(vmem_limit_bytes=(12 + count) << 20),
        cost_estimate=pl.CostEstimate(flops=4 * 10**9, bytes_accessed=4 << 20, transcendentals=0),
        name="early_filter",
    )(slots, *placed(inputs))


def late_filter_kernel(known, rows, where_ref, slots_ref, lo, raw, hi, early_ref, *refs):
    *grads, keep_ref, give_ref, grad, total, sem = refs
    pixels, lanes = raw.shape[1:]
    cols = pixels // rows
    pieces, taps, share, width = keep_ref.shape
    inner = pl.multiple_of(slots_ref[0] * share % lanes, 8)
    core = where_ref[1]
    for i in range(grad.shape[0]):
        start_map(grads, i, grad.at[i], sem)
    arrived(grad, sem)
    flat = [ref.reshape(raw.shape[0] * pixels, lanes) for ref in (lo, raw, hi)] + [cols]
    for t in range(9):
        terms = [
            tap_term(flat, slots_ref[known + i], t, grad.at[i]) for i in range(grad.shape[0])
        ]
        total[...] = functools.reduce(jnp.add, terms, early_ref[t])
        mine = total[pl.ds(inner, share), :]
        for i in range(pieces):
            even = mine[:, 2 * i * width : (2 * i + 1) * width]
            odd = mine[:, (2 * i + 1) * width : (2 * i + 2) * width]
            keep_ref[i, t] = jnp.where(core == 0, even, odd)
            give_ref[i, t] = jnp.where(core == 0, odd, even).astype(BF16)


def late_filter(where, slots, early, grads, known, rows, share, col_count):
    count = len(grads) - 1
    pixels, lanes = early[0].shape[1:]
    chans = early[3].shape[2]
    shape = (col_count // 2, 9, share, chans // col_count)
    return pl.pallas_call(
        functools.partial(late_filter_kernel, known, rows),
        out_shape=[jax.ShapeDtypeStruct(shape, F32), jax.ShapeDtypeStruct(shape, BF16)],
        in_specs=[SMEM, SMEM] + [VMEM] * 4 + [ANY] * len(grads),
        out_specs=[VMEM] * 2,
        scratch_shapes=[
            pltpu.VMEM((count, pixels, chans), BF16),
            pltpu.VMEM((lanes, chans), F32),
            pltpu.SemaphoreType.DMA,
        ],
        compiler_params=pltpu.CompilerParams(vmem_limit_bytes=(16 + count) << 20),
        cost_estimate=pl.CostEstimate(flops=2 * 10**9, bytes_accessed=4 << 20, transcendentals=0),
        name="late_filter",
    )(where, slots, *early, *placed(grads))


def edge_kernel(rows, feat_ref, grad_ref, first_ref, last_ref, maps, sems):
    cols = maps.shape[1] // rows
    loads = [
        pltpu.make_async_copy(ref, maps.at[n], sems.at[n])
        for n, ref in enumerate((feat_ref, grad_ref))
    ]
    for copy in loads:
        copy.start()
    for copy in loads:
        copy.wait()
    for out, at in ((first_ref, 0), (last_ref, cols - 1)):
        cells = [
            maps[n, h * cols + at : h * cols + at + 1, :].astype(F32)
            for n in range(2)
            for h in range(rows)
        ]
        out[...] = jnp.concatenate(cells, axis=0).astype(BF16)


def edges(feat, grad, rows):
    edge = jax.ShapeDtypeStruct((2 * rows, feat.shape[1]), BF16)
    return pl.pallas_call(
        functools.partial(edge_kernel, rows),
        out_shape=[edge, edge],
        in_specs=[ANY, ANY],
        out_specs=[VMEM, VMEM],
        scratch_shapes=[pltpu.VMEM((2,) + feat.shape, BF16), pltpu.SemaphoreType.DMA((2,))],
        name="edges",
    )(*placed([feat, grad]))


def ring_row(place, count):
    return jnp.where(place < count // 2, 2 * place, 2 * (count - 1 - place) + 1)


def ring_place(row, count):
    return jnp.where(row % 2 == 0, row // 2, count - 1 - row // 2)


def after(value, *earlier):
    return lax.optimization_barrier((value,) + earlier)[0]


def body(features, kernel, out_grad, projector, mixers):
    rows, cols, chans = features.shape
    row_count, col_count = lax.axis_size("rows"), lax.axis_size("cols")
    row, col = lax.axis_index("rows"), lax.axis_index("cols")
    rank = projector.shape[0]
    levels = col_count.bit_length() - 1
    half_way, pixels = row_count // 2, rows * cols

    order = list(range(0, row_count, 2)) + list(range(row_count - 1, 0, -2))
    east = [(i, i + 1) for i in range(col_count - 1)]
    west = [(j, i) for i, j in east]
    steps = [0] + [d for s in range(1, half_way) for d in (-s, s)] + [half_way]
    place = ring_place(row, row_count)
    slots = jnp.stack([ring_row((place + d) % row_count, row_count) for d in steps]).astype(jnp.int32)
    where = jnp.stack([row, col % 2, col, row]).astype(jnp.int32)

    def send(value, d):
        hop = [(order[i], order[(i + d) % row_count]) for i in range(row_count)]
        return lax.ppermute(value, "rows", hop)

    flat, own_grad = features.reshape(pixels, chans), out_grad.reshape(pixels, chans)
    first, last = edges(flat, own_grad, rows)
    near = [lax.ppermute(last, "cols", east), lax.ppermute(first, "cols", west)]
    packed = rank * pixels // chans
    tail = [projector[n : n + packed] for n in range(0, rank, packed)]
    message = jnp.concatenate([flat, jnp.concatenate(tail, axis=1)], axis=0)
    message = jnp.pad(message, ((0, 2 * rows), (0, 0)))
    message = lax.optimization_barrier(message)
    size = message.shape[0]
    sides = jnp.concatenate([x[:rows] for x in near])
    message = lax.dynamic_update_slice(message, sides, (size - 2 * rows, 0))
    feats = {0: message}
    beyond = []
    south = [(i, i + 1) for i in range(row_count - 1)]
    north = [(j, i) for i, j in south]
    for h, perm in ((rows - 1, south), (0, north)):
        cells = [x[n * rows + h : n * rows + h + 1] for n in range(2) for x in near]
        row_of = [x[h * cols : (h + 1) * cols] for x in (flat, own_grad)]
        parcel = jnp.concatenate(row_of + cells)
        parcel = jnp.pad(parcel, ((0, 2 * rows - len(cells)), (0, 0)))
        beyond.append(lax.ppermute(parcel, "rows", perm))
    for s in range(1, half_way):
        for d in (1, -1):
            feats[-s * d] = send(feats[(1 - s) * d], d)
    output, grad_features = convolutions(kernel, flat, own_grad, beyond, near, rows)
    feats[1 - half_way], feats[half_way - 1], output, grad_features = lax.optimization_barrier(
        (feats[1 - half_way], feats[half_way - 1], output, grad_features)
    )
    top, bottom = feats[1 - half_way], feats[half_way - 1]
    mid = size // 32 * 16
    feats[half_way] = [send(top[:mid], 1), send(bottom[mid:], -1)]
    grads = {0: own_grad}
    pairs = [(i, i ^ 1) for i in range(col_count)]
    met = lax.ppermute(top[:16, :128], "cols", pairs)
    late_grad, met, *_ = lax.optimization_barrier((own_grad, met, top, bottom))
    for d in (1, 2):
        grads[-d], grads[d] = send(late_grad, d), send(late_grad, -d)

    def listed(found, split=False):
        values = [found[d] for d in steps]
        return values[:-1] + list(values[-1]) if split else values

    feats = listed(feats, True)
    groups = [
        row_tree(slots, mixers[0], feats, start, rows, pixels)
        for start in range(0, row_count, GROUP)
    ]
    while len(groups) > 1:
        straight = where.at[0].set(0)
        groups = [
            merge(straight, mixers[0], groups[i], [groups[i + 1]])[0]
            for i in range(0, len(groups), 2)
        ]
    sketch = groups[0]

    def swap(value, level):
        return lax.ppermute(value, "cols", [(i, i ^ 1 << level) for i in range(col_count)])

    def turn(level):
        return where.at[0].set(col >> level & 1)

    swapped = swap(after(sketch, grads[1], grads[-1], grads[2], grads[-2]), 0)
    grads[-2], grads[2], _ = lax.optimization_barrier((grads[-2], grads[2], sketch))
    for s in range(3, half_way):
        for d in (1, -1):
            grads[-s * d] = send(grads[(1 - s) * d], d)
    result = merge(turn(0), mixers[1], sketch, [swapped])
    sketch, half = result
    top, bottom, _ = lax.optimization_barrier((grads[1 - half_way], grads[half_way - 1], half))
    split, known = pixels // 2, 5
    grads[half_way] = [send(top[:split], 1), send(bottom[split:], -1)]
    grads = listed(grads, True)
    share = chans // row_count
    early = early_filter(after(slots, half), feats, grads[:known], met, rows, share)
    terms, give = late_filter(where, slots, early, grads[known:], known, rows, share, col_count)
    filtered = give
    for level in range(levels):
        if level:
            pairs = terms.reshape((-1, 2) + terms.shape[1:])
            bit = col >> level & 1
            terms = lax.dynamic_index_in_dim(pairs, bit, 1, keepdims=False)
            give = lax.dynamic_index_in_dim(pairs, 1 - bit, 1, keepdims=False).astype(BF16)
        got = swap(give, level)
        if level < levels - 1:
            terms = terms + got.astype(F32)

    for level in range(1, levels):
        mine = swap(half, level)
        if level == 1:
            mine = after(mine, filtered)
        others = [mine, swap(mine, 0)]
        final = level == levels - 1
        share = (rank // col_count, sketch.shape[1] // row_count) if final else None
        result = merge(turn(level), mixers[1], sketch, others, share)
        sketch = result[0]
        if not final:
            half = result[1]
    grad_kernel = (terms + after(got, sketch).astype(F32))[0]
    return (
        output.reshape(features.shape),
        grad_features.reshape(features.shape),
        grad_kernel,
        sketch,
    )


def solution(mesh):
    in_specs = (P("rows", "cols", None), P(), P("rows", "cols", None), P("rows", "cols"), P())
    out_specs = (
        P("rows", "cols", None),
        P("rows", "cols", None),
        P(None, "rows", "cols"),
        P("cols", "rows"),
    )
    return jax.shard_map(body, mesh=mesh, in_specs=in_specs, out_specs=out_specs, check_vma=False)
```
